512 devices in a mesh: nodes: 128 (over z, x, core), feat: 4 (over y).
Axes of the slice: x: 4, y: 4, z: 16, core: 2. Of those that a mesh axis runs over, the one named last changes fastest.
Arguments:
- features: bfloat16 [65536, 128], P(('nodes', 'feat')), may hold values from -6 to 6
- block_vals: bfloat16 [512, 122, 128, 128], P(('nodes', 'feat')), may hold values from -3 to 3
- block_cols: int32 [512, 122], P(('nodes', 'feat')), may hold values from 0 to 127, as said below
- block_counts: int32 [512, 122], P(('nodes', 'feat')), may hold values from 1 to 256
- hub_parts: int32 [2], replicated, may hold values from 0 to 126, as said below
- send_blocks: int32 [512, 128], P(('nodes', 'feat')), may hold values from -1 to 3, as said below
- weight: bfloat16 [128, 256], replicated, may hold values from -0.5 to 0.5
- grad_out: bfloat16 [65536, 256], P(('nodes', 'feat')), may hold values from -0.0234375 to 0.0234375
Outputs:
- layer_out: bfloat16 [65536, 256], P(('nodes', 'feat'))
- weight_grad: float32 [128, 256], replicated
The draws below stay inside these ranges and needn't reach their ends.
Inputs may be any that keep to these rules, and one draw needn't show every extreme that they name: `hub_parts`: 2 distinct partitions. `block_cols`: slots below 2 hold a block of the row's own partition (0 to 3); the next 8 hold h * 4 + b for block b of partition hub_parts[h], and the hub slots of one device's 1 row blocks together name each of the 8 hub blocks once; the rest hold a partition p, neither the row's own nor a hub, for which send_blocks[p * 4 + f, g] is not -1 (g, f the row's partition and column). Every block that send_blocks names is read by some slot of the receiving device. `send_blocks`: entry [d, q] is -1, or a block of d's partition that d sends to the device of partition q in d's column; it is -1 where q is d's own partition, and in every column where d's partition is a hub. The number of partitions that one device reads from differs from device to device.
All inputs are finite; a program needn't handle non-finite values.
Results may differ from the reference program's by a relative error of at most 0.0057.
Values may be sent and summed in bfloat16 or wider, within the bound.
A program may use at most 64 MiB of HBM per device.

```python
import jax
import jax.numpy as jnp
from jax import lax

FIN = 128
HID = 256
BLK = 128
BLK_DEV = 1
KL = 2
KH = 8
KR = 112
K = 122
GB = 4
NHUB = 2
NBLK = 512
NODES = 65536
N_NODES = 128
N_FEAT = 4


def routing_plan(key):
    others = jax.random.permutation(jax.random.fold_in(key, 101), N_NODES - 2)[:NHUB - 1].astype(jnp.int32)
    hub_list = jnp.concatenate([jnp.full((1,), N_NODES - 2, jnp.int32), others]).astype(jnp.int32)
    device_count = N_NODES * N_FEAT
    read_slots = BLK_DEV * KR
    reader_group = jnp.arange(device_count, dtype=jnp.int32) // N_FEAT
    sources = jnp.arange(N_NODES, dtype=jnp.int32)
    hub_flag = jnp.any(sources[:, None] == hub_list[None, :], axis=1)
    blocked = hub_flag[None, :] | (sources[None, :] == reader_group[:, None])
    ranking = jax.random.randint(jax.random.fold_in(key, 102), (device_count, N_NODES), 0, 1 << 16) * N_NODES + sources[None, :]
    ranking = jnp.where(blocked, ranking + (1 << 16) * N_NODES, ranking)
    ranking = ranking.at[0, N_NODES - 1].set(-1)
    source_order = jnp.argsort(ranking, axis=1).astype(jnp.int32)
    eligible = N_NODES - jnp.sum(blocked.astype(jnp.int32), axis=1)
    fewest = max(1, 3 * read_slots // 4)
    read_count = jax.random.randint(jax.random.fold_in(key, 103), (device_count,), fewest, read_slots + 1)
    read_count = jnp.minimum(read_count, eligible)
    source_rank = jnp.argsort(source_order, axis=1).astype(jnp.int32)
    chosen = source_rank < read_count[:, None]
    block_pick = jax.random.randint(jax.random.fold_in(key, 104), (device_count, N_NODES), 0, GB)
    block_pick = block_pick.at[0, N_NODES - 1].set(GB - 1)
    read_list = jnp.where(chosen, block_pick, -1)
    grid_list = read_list.reshape(N_NODES, N_FEAT, N_NODES)
    send_list = jnp.transpose(grid_list, (2, 1, 0)).reshape(device_count, N_NODES)
    slot_ranking = jax.random.randint(jax.random.fold_in(key, 105), (device_count, read_slots), 0, 1 << 16) * read_slots + jnp.arange(read_slots, dtype=jnp.int32)[None, :]
    slot_order = jnp.argsort(slot_ranking, axis=1).astype(jnp.int32)
    wanted = slot_order % read_count[:, None]
    remote = jnp.take_along_axis(source_order, wanted, axis=1)
    remote = remote.reshape(device_count * BLK_DEV, KR)
    return (hub_list, send_list.astype(jnp.int32), remote.astype(jnp.int32))


def draw_hub_parts(key, part):
    hub_list, send_list, remote = routing_plan(key)
    return hub_list


def draw_send_blocks(key, part):
    hub_list, send_list, remote = routing_plan(key)
    return send_list


def draw_block_cols(key, part):
    hub_list, send_list, remote = routing_plan(key)
    key = jax.random.fold_in(key, 7)
    device_count = N_NODES * N_FEAT
    hub_total = NHUB * GB
    near_cols = jax.random.randint(jax.random.fold_in(key, 1), (NBLK, KL), 0, GB)
    hub_scores = jax.random.randint(jax.random.fold_in(key, 2), (device_count, hub_total), 0, 1 << 16) * hub_total + jnp.arange(hub_total, dtype=jnp.int32)[None, :]
    hub_cols = jnp.argsort(hub_scores, axis=1).astype(jnp.int32).reshape(device_count * BLK_DEV, KH)
    return jnp.concatenate([near_cols, hub_cols, remote], axis=1).astype(jnp.int32)


def with_ends(drawn, key, low, largest):
    extent = drawn.shape
    place = [jax.random.randint(jax.random.fold_in(key, axis), (), 0, extent[axis]) for axis in range(len(extent))]
    drawn = drawn.at[tuple(place)].set(low)
    longest = extent.index(max(extent))
    place[longest] = (place[longest] + 1) % extent[longest]
    return drawn.at[tuple(place)].set(largest)


def block_scale(key, extent, pieces, low, largest):
    def one(dim, parts):
        heights = jax.random.uniform(jax.random.fold_in(jax.random.fold_in(key, 6), dim), (parts,), jnp.float32, low / len(pieces), largest / len(pieces))
        return jnp.repeat(jnp.exp(heights), extent[dim] // parts).reshape((-1,) + (1,) * (len(extent) - dim - 1))

    level = one(*pieces[0])
    for cut in pieces[1:]:
        level = level * one(*cut)
    return level


def noise(key, shape, deviation, most, shards=(), kind=jnp.bfloat16):
    values = deviation * jax.random.normal(key, shape, jnp.float32)
    if shards:
        values = values * block_scale(key, shape, shards, -0.22, 0.18)
    return jnp.clip(values, -most, most).astype(kind)


def setup_inputs(seed: int = 0) -> dict:
    key_of = jax.random.split(jax.random.key(seed), 9)
    features = noise(key_of[0], (NODES, FIN), 1.0, 6.0, ((0, 512),))
    block_vals = noise(key_of[1], (NBLK, K, BLK, BLK), 0.5, 3.0, ((0, 512),))
    block_cols = draw_block_cols(jax.random.fold_in(key_of[8], 71), 0)
    block_counts = with_ends(jax.random.randint(key_of[3], (NBLK, K), 1, 257), jax.random.fold_in(key_of[3], 1), 1, 256).astype(jnp.int32)
    hub_parts = draw_hub_parts(jax.random.fold_in(key_of[8], 71), 0)
    send_blocks = draw_send_blocks(jax.random.fold_in(key_of[8], 71), 0)
    weight = noise(key_of[6], (FIN, HID), FIN ** -0.5, 0.5)
    grad_out = noise(key_of[7], (NODES, HID), NODES ** -0.5, 0.0234375, ((0, 512),))
    return dict(features=features, block_vals=block_vals, block_cols=block_cols, block_counts=block_counts, hub_parts=hub_parts, send_blocks=send_blocks, weight=weight, grad_out=grad_out)


def resolve(block_cols, hub_parts, send_blocks):
    row_block = jnp.arange(NBLK, dtype=jnp.int32)
    device = row_block // BLK_DEV
    group_id = (device // N_FEAT)[:, None]
    column = (device % N_FEAT)[:, None]
    near_ids = group_id * GB + block_cols[:, :KL]
    hub_slot = block_cols[:, KL:KL + KH]
    hub_ids = hub_parts[hub_slot // GB] * GB + hub_slot % GB
    source = block_cols[:, KL + KH:]
    sent_block = send_blocks[source * N_FEAT + column, group_id]
    far_ids = source * GB + sent_block
    return jnp.concatenate([near_ids, hub_ids, far_ids], axis=1).astype(jnp.int32)


def reference(features, block_vals, block_cols, block_counts, hub_parts, send_blocks, weight, grad_out):
    block_ids = resolve(block_cols, hub_parts, send_blocks)
    counts = block_counts.astype(jnp.float32)
    fraction = counts / jnp.sum(counts, axis=1, keepdims=True)
    blocks = features.reshape(NBLK, BLK, FIN)

    def per_block(packed):
        tile_vals, tile_ids, share_row = packed
        scaled = (share_row[:, None, None] * tile_vals.astype(jnp.float32)).astype(jnp.bfloat16)
        sources = blocks[tile_ids]
        return jnp.einsum("krc,kcf->rf", scaled.astype(jnp.float32), sources.astype(jnp.float32))

    hidden = lax.map(per_block, (block_vals, block_ids, fraction))
    hidden = hidden.reshape(NODES, FIN).astype(jnp.bfloat16)
    layer_out = jnp.dot(hidden, weight, preferred_element_type=jnp.float32).astype(jnp.bfloat16)
    weight_grad = jnp.dot(hidden.T, grad_out, preferred_element_type=jnp.float32)
    return layer_out, weight_grad
```

```python
import functools

import jax
import jax.numpy as jnp
from jax import lax
from jax.experimental import pallas as pl
from jax.experimental.pallas import tpu as pltpu
from jax.sharding import PartitionSpec as P

KL, KH, K = 2, 8, 122
BLK, HID = 128, 256
MESH = pl.DeviceIdType.MESH
A = pl.ds(0, 16)
ROWS = (pl.ds(16, 48), pl.ds(64, 64))
ALL = slice(None)
LAST = 8
LAG = 2
SCALE_STEPS = 10


def where_am_i():
    n = lax.axis_index("nodes")
    return n // 8, (n // 2) % 4, n % 2, lax.axis_index("feat")


def device(z, x, c, y):
    return ((z % 16) * 8 + (x % 4) * 2 + c, y % 4)


def kernel(
    feat_ref, vals_hbm, cols_ref, counts_ref, hubs_ref, send_ref, weight_ref, grad_ref,
    layer_ref, wgrad_ref,
    G, S, S_sm, vals, frac_v, frac, index, srow, stride, W, R1, R2, Wout,
    local_sem, small_send, small_recv, a_send, a_recv, z_send, z_recv,
    one_send, one_recv, two_send, two_recv, c_send, c_recv, s_send, s_recv, r_send, r_recv,
):
    z, x, c, y = where_am_i()
    first = c == 0

    def at_u(d):
        return device(z, x + jnp.where(first, d, 0), c, y + jnp.where(first, 0, d))

    def at_v(d):
        return device(z, x + jnp.where(first, 0, d), c, y + jnp.where(first, d, 0))

    at_uv = (at_u, at_v)
    z_peer = (device(z + 1, x, c, y), device(z + 15, x, c, y))
    other = device(z, x, 1 - c, y)

    load = pltpu.make_async_copy(vals_hbm.at[0], vals, local_sem.at[0])
    load.start()
    G[0, 0, 0, 0, 0] = feat_ref[...]
    S[0, 0, 0, 0] = send_ref[...]

    barrier = pltpu.get_barrier_semaphore()
    greeted = [device(z, x + d, c, y) for d in (1, 2, 3)]
    greeted += [device(z, x, c, y + d) for d in (1, 2, 3)]
    greeted += [*z_peer, other]
    for peer in greeted:
        pl.semaphore_signal(barrier, inc=1, device_id=peer, device_id_type=MESH)
    counts = counts_ref[...].astype(jnp.float32)
    frac_v[...] = counts / jnp.sum(counts, axis=1, keepdims=True)
    pl.semaphore_wait(barrier, len(greeted))

    pending = []

    def send(src, dst, ssem, rsem, peer):
        copy = pltpu.make_async_remote_copy(
            src_ref=src, dst_ref=dst, send_sem=ssem, recv_sem=rsem,
            device_id=peer, device_id_type=MESH,
        )
        copy.start()
        pending.append(copy)
        return copy

    def arrived(copies):
        for copy in copies:
            copy.wait_recv()

    def retire(keep):
        while len(pending) > keep:
            pending.pop(0).wait_send()

    own = G.at[0, 0, 0]
    small_v = [
        send(own.at[0, 0, pl.ds(0, 64)], own.at[0, d, pl.ds(0, 64)],
             small_send.at[1, d], small_recv.at[1, d], at_v(d))
        for d in (1, 3, 2)
    ]
    small_u = [
        send(own.at[0, 0, ROWS[1]], own.at[d, 0, ROWS[1]],
             small_send.at[0, d], small_recv.at[0, d], at_u(d))
        for d in (1, 3, 2)
    ]
    frac_copy = pltpu.make_async_copy(frac_v, frac, local_sem.at[1])
    frac_copy.start()

    def strip(p, k, way, place):
        if p == 0:
            return G.at[0, k, way, place, ALL, ROWS[0]]
        return G.at[0, k, way, ALL, place, ROWS[1]]

    def slot(k, way):
        return (0, 1) if k == LAST else (k, way)

    def z_forward(p, k):
        copies = []
        for way in (0, 1):
            if k + 1 == LAST and way == 1:
                continue
            kk, ww = slot(k + 1, way)
            src = strip(p, k, way if k else 0, 0)
            copies.append(send(src, strip(p, kk, ww, 0), z_send.at[p, way, k], z_recv.at[p, way, k], z_peer[way]))
        return copies

    def a_forward(k):
        copies = []
        for way in (0, 1):
            if k + 1 == LAST and way == 0:
                continue
            kk, ww = slot(k + 1, way)
            src = G.at[0, k, way if k else 0, ALL, ALL, A]
            dst = G.at[0, kk, ww, ALL, ALL, A]
            copies.append(send(src, dst, z_send.at[2, way, k], z_recv.at[2, way, k], z_peer[way]))
        return copies

    def s_forward(k):
        copies = []
        for way in (0, 1):
            if k + 1 == LAST and way == 0:
                continue
            kk, ww = slot(k + 1, way)
            src = S.at[0, 0, k, way if k else 0]
            copies.append(send(src, S.at[0, 0, kk, ww], z_send.at[3, way, k], z_recv.at[3, way, k], z_peer[way]))
        return copies

    def pair(k):
        if k == 0:
            return 0, 0
        if k == LAST:
            return 0, 1
        return k, ALL

    def large_one(p, k):
        kk, ww = pair(k)
        return [
            send(strip(p, kk, ww, 0), strip(p, kk, ww, d), one_send.at[p, i, k], one_recv.at[p, i, k], at_uv[p](d))
            for i, d in enumerate((1, 3))
        ]

    def large_two(p, k):
        copies = []
        for i, d in enumerate((1, 3)):
            if k == 0 and i == 1 or k == LAST and i == 0:
                continue
            kk = 0 if k == LAST else k
            copies.append(
                send(strip(p, kk, i, d), strip(p, kk, i, 2), two_send.at[p, i, k], two_recv.at[p, i, k], at_uv[p](d))
            )
        return copies

    def across(k):
        kk, ww = pair(k)
        rows = pl.ds(16, 112)
        return [send(G.at[0, kk, ww, ALL, ALL, rows], G.at[1, kk, ww, ALL, ALL, rows], c_send.at[0, k], c_recv.at[0, k], other)]

    def a_across(k):
        kk, ww = pair(k)
        return [send(G.at[0, kk, ww, ALL, ALL, A], G.at[1, kk, ww, ALL, ALL, A], c_send.at[1, k], c_recv.at[1, k], other)]

    s_moves = {1: s_forward(0)}

    def base_of(p):
        away = (z - p // 8) % 16
        cell = jnp.where(away < 8, 2 * away, (33 - 2 * away) % 16)
        core = p % 2
        rel = jnp.where(core == c, 0, 1)
        along = (x - (p // 2) % 4) % 4
        base = (rel * 16 + cell) * 16 + along * jnp.where(core == 0, 4, 1)
        return base, jnp.where(core == 0, 1, 4), (rel * 4 + along) * 16 + cell

    mine = z * 8 + x * 2 + c

    def near(s, _):
        base, step, _row = base_of(mine)
        index[s] = base + ((y - cols_ref[0, s]) % 4) * step
        return 0

    def hub(s, _):
        v = cols_ref[0, s]
        base, step, _row = base_of(hubs_ref[v // 4])
        index[s] = base + ((y - v % 4) % 4) * step
        return 0

    def far(s, _):
        base, step, row = base_of(cols_ref[0, s])
        index[s] = base
        stride[s] = step
        srow[s] = row
        return 0

    lax.fori_loop(0, KL, near, 0)
    lax.fori_loop(KL, KL + KH, hub, 0)
    lax.fori_loop(KL + KH, K, far, 0)

    frac_copy.wait()
    arrived(small_v)
    z_moves = {}
    ones = {}
    twos = {}
    crossing = []
    z_moves[0, 1] = z_forward(0, 0)
    ones[0, 0] = large_one(0, 0)
    a_small = [
        send(own.at[0, ALL, A], own.at[d, ALL, A], a_send.at[d], a_recv.at[d], at_u(d)) for d in (1, 3, 2)
    ]
    arrived(small_u)
    z_moves[1, 1] = z_forward(1, 0)
    ones[1, 0] = large_one(1, 0)
    load.wait()

    def scale(part):
        def one(s, _):
            vals[s] = (frac[0, s] * vals[s].astype(jnp.float32)).astype(jnp.bfloat16)
            return 0

        per = (K + SCALE_STEPS - 1) // SCALE_STEPS
        if part < SCALE_STEPS:
            lax.fori_loop(part * per, min(K, (part + 1) * per), one, 0)

    a_moves = {}
    s_x = s_c = None
    for k in range(1, LAST + 4 + LAG):
        scale(k - 1)
        for p in (0, 1):
            if k <= LAST:
                arrived(z_moves[p, k])
                if k < LAST:
                    z_moves[p, k + 1] = z_forward(p, k)
                ones[p, k] = large_one(p, k)
        if k <= LAST:
            arrived(s_moves[k])
            if k < LAST:
                s_moves[k + 1] = s_forward(k)
            else:
                s_x = [
                    send(S.at[0, 0], S.at[0, d], s_send.at[d], s_recv.at[d], device(z, x + d, c, y))
                    for d in (1, 2, 3)
                ]
        for p in (0, 1):
            if k - 1 <= LAST:
                arrived(ones[p, k - 1])
                twos[p, k - 1] = large_two(p, k - 1)
        step = k - LAG
        if step == 0:
            arrived(a_small)
            a_moves[1] = a_forward(0)
            crossing += a_across(0)
        elif 1 <= step <= LAST:
            arrived(a_moves[step])
            if step < LAST:
                a_moves[step + 1] = a_forward(step)
            crossing += a_across(step)
        if 0 <= k - 2 <= LAST:
            arrived(twos[0, k - 2] + twos[1, k - 2])
            crossing += across(k - 2)
        if k == LAST + 1:
            arrived(s_x)
            s_c = [send(S.at[0], S.at[1], s_send.at[0], s_recv.at[0], other)]
        if k == LAST + 2:
            arrived(s_c)
            s_copy = pltpu.make_async_copy(S, S_sm, local_sem.at[2])
            s_copy.start()
        retire(48)

    s_copy.wait()

    def resolve(s, _):
        row = srow[s]
        sent = S_sm[row // 64, (row // 16) % 4, (row // 2) % 8, row % 2, 0, mine]
        index[s] = index[s] + ((y - sent) % 4) * stride[s]
        return 0

    lax.fori_loop(KL + KH, K, resolve, 0)
    arrived(crossing)

    def block(s):
        i = index[s]
        return G[i // 256, (i // 32) % 8, (i // 16) % 2, (i // 4) % 4, i % 4]

    def pair_dot(s):
        left = jnp.concatenate([vals[s], vals[s + 1]], axis=1)
        right = jnp.concatenate([block(s), block(s + 1)], axis=0)
        return jnp.dot(left, right, preferred_element_type=jnp.float32)

    def quad(i, total):
        s = i * 8
        return total + ((pair_dot(s) + pair_dot(s + 2)) + (pair_dot(s + 4) + pair_dot(s + 6)))

    total = lax.fori_loop(0, 15, quad, pair_dot(120))
    hidden = total.astype(jnp.bfloat16)
    grad = lax.dot_general(hidden, grad_ref[...], (((0,), (0,)), ((), ())), preferred_element_type=jnp.float32)
    for i in range(16):
        for h in range(2):
            W[2 * i + h] = grad[8 * i : 8 * i + 8, 128 * h : 128 * h + 128]

    def plane_peer(j):
        px, py, pc = (x + j // 8) % 4, (y + (j // 2) % 4) % 4, (c + j % 2) % 2
        return device(z, px, pc, py), px * 8 + py * 2 + pc

    def plane_copy(j, scatter):
        peer, tile = plane_peer(j)
        me = x * 8 + y * 2 + c
        src, dst = (W.at[tile], R1.at[j]) if scatter else (Wout.at[me], Wout.at[me])
        which = 0 if scatter else 2
        return pltpu.make_async_remote_copy(
            src_ref=src, dst_ref=dst, send_sem=r_send.at[which], recv_sem=r_recv.at[which],
            device_id=peer, device_id_type=MESH,
        )

    def z_copy(j):
        return pltpu.make_async_remote_copy(
            src_ref=R2.at[0], dst_ref=R2.at[j], send_sem=r_send.at[1], recv_sem=r_recv.at[1],
            device_id=device(z + j, x, c, y), device_id_type=MESH,
        )

    def start_all(make, count):
        def go(j, _):
            make(j).start()
            return 0

        lax.fori_loop(1, count, go, 0)

    def wait_all(ref, count, sem):
        part = ref.at[pl.ds(1, count - 1)]
        pltpu.make_async_copy(part, part, sem).wait()

    me = x * 8 + y * 2 + c
    start_all(functools.partial(plane_copy, scatter=True), 32)
    layer_ref[...] = jnp.dot(hidden, weight_ref[...], preferred_element_type=jnp.float32).astype(jnp.bfloat16)
    R1[0] = W[me]
    wait_all(R1, 32, r_recv.at[0])
    R2[0] = jnp.sum(R1[...], axis=0)
    start_all(z_copy, 16)
    retire(0)
    wait_all(R2, 16, r_recv.at[1])
    wait_all(R2, 16, r_send.at[1])
    Wout[me] = jnp.sum(R2[...], axis=0)
    start_all(functools.partial(plane_copy, scatter=False), 32)
    wait_all(R1, 32, r_send.at[0])
    wait_all(Wout, 32, r_recv.at[2])
    for i in range(16):
        for h in range(2):
            wgrad_ref[8 * i : 8 * i + 8, 128 * h : 128 * h + 128] = Wout[2 * i + h]
    wait_all(Wout, 32, r_send.at[2])


def per_device(features, block_vals, block_cols, block_counts, hub_parts, send_blocks, weight, grad_out):
    vmem = pl.BlockSpec(memory_space=pltpu.VMEM)
    smem = pl.BlockSpec(memory_space=pltpu.SMEM)
    dma = pltpu.SemaphoreType.DMA
    return pl.pallas_call(
        kernel,
        out_shape=(
            jax.ShapeDtypeStruct((BLK, HID), jnp.bfloat16),
            jax.ShapeDtypeStruct((BLK, HID), jnp.float32),
        ),
        in_specs=[vmem, pl.BlockSpec(memory_space=pl.ANY), smem, vmem, smem, vmem, vmem, vmem],
        out_specs=(vmem, vmem),
        scratch_shapes=[
            pltpu.VMEM((2, 8, 2, 4, 4, BLK, BLK), jnp.bfloat16),
            pltpu.VMEM((2, 4, 8, 2, 1, BLK), jnp.int32),
            pltpu.SMEM((2, 4, 8, 2, 1, BLK), jnp.int32),
            pltpu.VMEM((K, BLK, BLK), jnp.bfloat16),
            pltpu.VMEM((1, K), jnp.float32),
            pltpu.SMEM((1, K), jnp.float32),
            pltpu.SMEM((K,), jnp.int32),
            pltpu.SMEM((K,), jnp.int32),
            pltpu.SMEM((K,), jnp.int32),
            pltpu.VMEM((32, 8, BLK), jnp.float32),
            pltpu.VMEM((32, 8, BLK), jnp.float32),
            pltpu.VMEM((16, 8, BLK), jnp.float32),
            pltpu.VMEM((32, 8, BLK), jnp.float32),
            dma((3,)),
            dma((2, 4)), dma((2, 4)),
            dma((4,)), dma((4,)),
            dma((4, 2, 8)), dma((4, 2, 8)),
            dma((2, 2, 9)), dma((2, 2, 9)),
            dma((2, 2, 9)), dma((2, 2, 9)),
            dma((2, 9)), dma((2, 9)),
            dma((4,)), dma((4,)),
            dma((3,)), dma((3,)),
        ],
        compiler_params=pltpu.CompilerParams(
            collective_id=0, has_side_effects=True, vmem_limit_bytes=40 << 20
        ),
    )(features, block_vals, block_cols, block_counts, hub_parts, send_blocks, weight, grad_out)


def solution(mesh):
    placed = (
        P(("nodes", "feat"), None),
        P(("nodes", "feat"), None, None, None),
        P(("nodes", "feat"), None),
        P(("nodes", "feat"), None),
        P(),
        P(("nodes", "feat"), None),
        P(),
        P(("nodes", "feat"), None),
    )
    return jax.shard_map(
        per_device,
        mesh=mesh,
        in_specs=placed,
        out_specs=(P(("nodes", "feat"), None), P()),
        check_vma=False,
    )
```

```python
import math

import jax
import jax.numpy as jnp
from jax import lax
from jax.experimental import pallas as pl
from jax.experimental.pallas import tpu as pltpu
from jax.sharding import PartitionSpec as P

KL, KH, K = 2, 8, 122
BLK, HID = 128, 256
MESH = pl.DeviceIdType.MESH
ALL = slice(None)
A_ROWS = pl.ds(0, 16)
ROWS = (pl.ds(16, 48), pl.ds(64, 64))
HALVES = (pl.ds(0, 2), pl.ds(2, 2))
LAST = 8
A_LAG = 1
TWO_LAG = 1
ACROSS_LAG = 3
CHUNK = 16
WORK_STEPS = 8
VMEM_BYTES = 63 << 20


def where_am_i():
    n = lax.axis_index("nodes")
    return n // 8, (n // 2) % 4, n % 2, lax.axis_index("feat")


def device(z, x, c, y):
    return ((z % 16) * 8 + (x % 4) * 2 + c, y % 4)


def kernel(
    feat_hbm, vals_hbm, cols_hbm, counts_hbm, hubs_hbm, send_hbm, weight_hbm, grad_hbm,
    layer_hbm, wgrad_hbm,
    G, S, S_sm, vals, cols, counts_v, hubs, weight, grad_out, frac_v, frac, index, srow, stride,
    layer, W, R1, R2, total_tile,
    local_sem, sent_sem, small_recv, z_recv, one_recv, two_recv, c_recv, s_sent, s_recv, r_recv,
):
    z, x, c, y = where_am_i()
    first = c == 0

    def at_u(d):
        return device(z, x + jnp.where(first, d, 0), c, y + jnp.where(first, 0, d))

    def at_v(d):
        return device(z, x + jnp.where(first, 0, d), c, y + jnp.where(first, d, 0))

    at_uv = (at_u, at_v)
    z_peer = (device(z + 1, x, c, y), device(z + 15, x, c, y))
    other = device(z, x, 1 - c, y)

    barrier = pltpu.get_barrier_semaphore()
    greeted = [device(z, x + d, c, y) for d in (1, 2, 3)]
    greeted += [device(z, x, c, y + d) for d in (1, 2, 3)]
    greeted += [*z_peer, other]
    for peer in greeted:
        pl.semaphore_signal(barrier, inc=1, device_id=peer, device_id_type=MESH)

    def load(i, src, dst):
        copy = pltpu.make_async_copy(src, dst, local_sem.at[i])
        copy.start()
        return copy

    own = G.at[0, 0, 0]
    got_feat = load(0, feat_hbm, own.at[0, 0])
    got_send = load(1, send_hbm, S.at[8, 0, 0])
    got_counts = load(2, counts_hbm, counts_v)
    got_cols = load(3, cols_hbm, cols)
    got_hubs = load(4, hubs_hbm, hubs)
    got_vals = load(5, vals_hbm.at[0], vals)
    got_weight = load(6, weight_hbm, weight)
    got_grad = load(7, grad_hbm, grad_out)
    got_counts.wait()
    counts = counts_v[...].astype(jnp.float32)
    frac_v[...] = counts / jnp.sum(counts, axis=1, keepdims=True)
    got_frac = load(8, frac_v, frac)
    got_feat.wait()
    got_send.wait()
    pl.semaphore_wait(barrier, len(greeted))

    lines = G.reshape(512 * BLK, BLK)
    sent_rows = []

    def wait_rows(sem, rows):
        part = lines.at[pl.ds(0, rows)]
        pltpu.make_async_copy(part, part, sem).wait()

    def send(src, dst, sem, peer, near_core=False):
        rows = math.prod(src.shape[:-1])
        pltpu.make_async_remote_copy(
            src_ref=src, dst_ref=dst, send_sem=sent_sem.at[int(near_core)], recv_sem=sem,
            device_id=peer, device_id_type=MESH,
        ).start()
        if not near_core:
            sent_rows.append(rows)
        return sem, rows

    def arrived(group):
        wait_rows(group[0][0], sum(rows for _, rows in group))

    front = pl.ds(0, 64)
    small_v = {
        d: send(own.at[0, 0, front], own.at[0, d, front], small_recv.at[0 if d == 1 else 1], at_v(d))
        for d in (1, 3, 2)
    }
    small_u = {
        d: send(own.at[0, 0, ROWS[1]], own.at[d, 0, ROWS[1]], small_recv.at[2 if d == 1 else 3], at_u(d))
        for d in (1, 3, 2)
    }
    s_rows = []

    def s_send(i, peer, src, dst):
        pltpu.make_async_remote_copy(
            src_ref=src, dst_ref=dst, send_sem=s_sent.at[0], recv_sem=s_recv.at[i],
            device_id=peer, device_id_type=MESH,
        ).start()
        s_rows.append(math.prod(src.shape[:-2]))
        return i, s_rows[-1]

    def s_wait(sem, rows):
        part = S.reshape(128, 1, BLK).at[pl.ds(0, rows)]
        pltpu.make_async_copy(part, part, sem).wait()

    def s_arrived(group):
        s_wait(s_recv.at[group[0][0]], sum(rows for _, rows in group))

    def s_shift(i, d, low, count):
        src, dst = S.at[pl.ds(8 + low, count)], S.at[pl.ds(8 + low + d, count)]
        return s_send(i, device(z + d + 16, x, c, y), src, dst)

    s_moves = [s_send(0, device(z, x + d, c, y), S.at[8, 0, 0], S.at[8, 0, d]) for d in (1, 3, 2)]

    def strip(p, k, way, place, half=ALL):
        if p == 0:
            return G.at[0, k, way, place, half, ROWS[0]]
        if p == 1:
            return G.at[0, k, way, half, place, ROWS[1]]
        return G.at[0, k, way, half, ALL, A_ROWS]

    def slot(k, way):
        return (0, 1) if k == LAST else (k, way)

    def z_forward(p, k, h):
        copies = []
        for way in (0, 1):
            if k + 1 == LAST and way == (0 if p == 2 else 1):
                continue
            kk, ww = slot(k + 1, way)
            src = strip(p, k, way if k else 0, 0, HALVES[h])
            dst = strip(p, kk, ww, 0, HALVES[h])
            copies.append(send(src, dst, z_recv.at[p, h, k], z_peer[way]))
        return copies

    def pair(k):
        if k == 0:
            return 0, 0
        if k == LAST:
            return 0, 1
        return k, ALL

    def large_one(p, k):
        kk, ww = pair(k)
        return [
            send(strip(p, kk, ww, 0), strip(p, kk, ww, d), one_recv.at[p, k], at_uv[p](d))
            for i, d in enumerate((1, 3))
        ]

    def large_two(p, k):
        copies = []
        for i, d in enumerate((1, 3)):
            if k == 0 and i == 1 or k == LAST and i == 0:
                continue
            kk = 0 if k == LAST else k
            copies.append(
                send(strip(p, kk, i, d), strip(p, kk, i, 2), two_recv.at[k], at_uv[p](d))
            )
        return copies

    def across(k):
        kk, ww = pair(k)
        rows = pl.ds(16, 112)
        return [send(G.at[0, kk, ww, ALL, ALL, rows], G.at[1, kk, ww, ALL, ALL, rows], c_recv.at[0], other, True)]

    def a_across(k):
        kk, ww = pair(k)
        return [send(G.at[0, kk, ww, ALL, ALL, A_ROWS], G.at[1, kk, ww, ALL, ALL, A_ROWS], c_recv.at[0], other, True)]

    def base_of(p):
        away = (z - (p >> 3)) & 15
        cell = jnp.where(away < 8, 2 * away, (33 - 2 * away) & 15)
        core = p & 1
        rel = core ^ c
        along = (x - ((p >> 1) & 3)) & 3
        base = (rel * 16 + cell) * 16 + along * jnp.where(core == 0, 4, 1)
        return base, jnp.where(core == 0, 1, 4), ((away + 8) & 15) * 8 + rel * 4 + along

    mine = z * 8 + x * 2 + c

    def near(s, _):
        base, step, _row = base_of(mine)
        index[s] = base + ((y - cols[0, s]) & 3) * step
        return 0

    def hub(s, _):
        v = cols[0, s]
        base, step, _row = base_of(hubs[v >> 2])
        index[s] = base + ((y - v) & 3) * step
        return 0

    def far(s, _):
        base, step, row = base_of(cols[0, s])
        index[s] = base
        stride[s] = step
        srow[s] = row
        return 0

    def resolve(s, _):
        row = srow[s]
        sent = S_sm[row >> 3, (row >> 2) & 1, row & 3, 0, mine]
        index[s] = index[s] + ((y - sent) & 3) * stride[s]
        return 0

    def scale(s, _):
        vals[s] = (frac[0, s] * vals[s].astype(jnp.float32)).astype(jnp.bfloat16)
        return 0

    def portion(body, low, high, part, parts):
        per = (high - low + parts - 1) // parts
        if 0 <= part < parts:
            lax.fori_loop(low + part * per, min(high, low + (part + 1) * per), body, 0)

    z_moves = {}
    ones = {}
    twos = {}
    crossing = []
    arrived([small_v[1]])
    z_moves[0, 0, 1] = z_forward(0, 0, 0)
    arrived([small_v[3], small_v[2]])
    z_moves[0, 1, 1] = z_forward(0, 0, 1)
    ones[0, 0] = large_one(0, 0)
    arrived([small_u[1]])
    z_moves[1, 0, 1] = z_forward(1, 0, 0)
    arrived([small_u[3], small_u[2]])
    z_moves[1, 1, 1] = z_forward(1, 0, 1)
    ones[1, 0] = large_one(1, 0)
    a_small = [
        send(own.at[0, ALL, A_ROWS], own.at[d, ALL, A_ROWS], small_recv.at[4], at_u(d)) for d in (1, 3, 2)
    ]
    got_cols.wait()
    got_hubs.wait()
    lax.fori_loop(0, KL, near, 0)
    lax.fori_loop(KL, KL + KH, hub, 0)
    s_arrived(s_moves)
    s_moves = [s_send(1, other, S.at[8, 0], S.at[8, 1])]
    got_frac.wait()
    got_vals.wait()
    got_s = None
    for k in range(1, LAST + ACROSS_LAG + 1):
        portion(scale, 0, K, k - 1, WORK_STEPS)
        portion(far, KL + KH, K, k - 1, 4)
        portion(resolve, KL + KH, K, k - 9, 2)
        for p in (0, 1):
            if k <= LAST:
                for h in (0, 1):
                    arrived(z_moves[p, h, k])
                    if k < LAST:
                        z_moves[p, h, k + 1] = z_forward(p, k, h)
                ones[p, k] = large_one(p, k)
        step = k - A_LAG
        if step == 0:
            arrived(a_small)
            for h in (0, 1):
                z_moves[2, h, 1] = z_forward(2, 0, h)
            crossing += a_across(0)
        elif 1 <= step <= LAST:
            for h in (0, 1):
                arrived(z_moves[2, h, step])
                if step < LAST:
                    z_moves[2, h, step + 1] = z_forward(2, step, h)
            crossing += a_across(step)
        late = k - TWO_LAG
        if 0 <= late <= LAST:
            for p in (0, 1):
                arrived(ones[p, late])
                twos[p, late] = large_two(p, late)
        late = k - ACROSS_LAG
        if 0 <= late <= LAST:
            arrived(twos[0, late] + twos[1, late])
            crossing += across(late)
        if k == 1:
            s_arrived(s_moves)
            s_moves = [s_shift(2, 1, 0, 1), s_shift(2, -1, 0, 1)]
        if k == 3:
            s_arrived(s_moves)
            s_moves = [s_shift(3, 3, -1, 3), s_shift(3, -3, -1, 3)]
        if k == 5:
            s_arrived(s_moves)
            s_moves = [s_shift(4, 4, 1, 3), s_shift(4, -4, -4, 4)]
        if k == 7:
            s_arrived(s_moves)
            got_s = load(9, S, S_sm)
        if k == 8:
            got_s.wait()

    arrived(crossing)

    flat = G.reshape(512, BLK, BLK)

    def chunk_dot(s, count):
        left = jnp.concatenate([vals[s + i] for i in range(count)], axis=1)
        right = jnp.concatenate([flat[index[s + i]] for i in range(count)], axis=0)
        return jnp.dot(left, right, preferred_element_type=jnp.float32)

    rest = K % CHUNK
    total = lax.fori_loop(
        0, K // CHUNK, lambda i, acc: acc + chunk_dot(i * CHUNK, CHUNK), chunk_dot(K - rest, rest)
    )
    hidden = total.astype(jnp.bfloat16)
    got_grad.wait()
    grad = lax.dot_general(hidden, grad_out[...], (((0,), (0,)), ((), ())), preferred_element_type=jnp.float32)
    for i in range(16):
        for h in range(2):
            W[2 * i + h] = grad[8 * i : 8 * i + 8, 128 * h : 128 * h + 128]

    me = x * 8 + y * 2 + c
    plane = sorted(
        ((dx, dy, dc) for dx in range(4) for dy in range(4) for dc in range(2) if (dx, dy, dc) != (0, 0, 0)),
        key=lambda d: -(min(d[0], 4 - d[0]) + min(d[1], 4 - d[1])) * 2 - d[2],
    )

    def at_tile(tile):
        rows = pl.ds(pl.multiple_of(8 * (tile // 2), 8), 8)
        return wgrad_hbm.at[rows, pl.ds(pl.multiple_of(BLK * (tile % 2), BLK), BLK)]

    def tile_send(src, dst, sem, peer):
        pltpu.make_async_remote_copy(
            src_ref=src, dst_ref=dst, send_sem=sent_sem.at[0], recv_sem=sem,
            device_id=peer, device_id_type=MESH,
        ).start()
        sent_rows.append(16)

    def plane_send(scatter):
        for j, (dx, dy, dc) in enumerate(plane):
            px, py, pc = (x + dx) % 4, (y + dy) % 4, (c + dc) % 2
            peer = device(z, px, pc, py)
            if scatter:
                tile_send(W.at[px * 8 + py * 2 + pc], R1.at[j + 1], r_recv.at[0], peer)
            else:
                tile_send(total_tile, at_tile(me), r_recv.at[2], peer)

    def wait_tiles(sem, count):
        part = W.at[pl.ds(0, count)]
        pltpu.make_async_copy(part, part, sem).wait()

    plane_send(True)
    got_weight.wait()
    layer[...] = jnp.dot(hidden, weight[...], preferred_element_type=jnp.float32).astype(jnp.bfloat16)
    put_layer = load(0, layer, layer_hbm)
    R1[0] = W[me]
    wait_tiles(r_recv.at[0], 31)
    R2[0] = jnp.sum(R1[...], axis=0)
    for j in (8, 7, 9, 6, 10, 5, 11, 4, 12, 3, 13, 2, 14, 1, 15):
        tile_send(R2.at[0], R2.at[j], r_recv.at[1], device(z + j, x, c, y))
    s_wait(s_sent.at[0], sum(s_rows))
    put_layer.wait()
    wait_tiles(r_recv.at[1], 15)
    total_tile[...] = jnp.sum(R2[...], axis=0)
    plane_send(False)
    put_tile = load(1, total_tile, at_tile(me))
    put_tile.wait()
    wait_tiles(r_recv.at[2], 31)
    wait_rows(sent_sem.at[0], sum(sent_rows))
    wait_rows(sent_sem.at[1], sum(rows for _, rows in crossing))


def per_device(features, block_vals, block_cols, block_counts, hub_parts, send_blocks, weight, grad_out):
    dma = pltpu.SemaphoreType.DMA
    return pl.pallas_call(
        kernel,
        out_shape=(
            jax.ShapeDtypeStruct((BLK, HID), jnp.bfloat16),
            jax.ShapeDtypeStruct((BLK, HID), jnp.float32),
        ),
        in_specs=[pl.BlockSpec(memory_space=pl.ANY)] * 8,
        out_specs=(pl.BlockSpec(memory_space=pl.ANY),) * 2,
        scratch_shapes=[
            pltpu.VMEM((2, 8, 2, 4, 4, BLK, BLK), jnp.bfloat16),
            pltpu.VMEM((16, 2, 4, 1, BLK), jnp.int32),
            pltpu.SMEM((16, 2, 4, 1, BLK), jnp.int32),
            pltpu.VMEM((K, BLK, BLK), jnp.bfloat16),
            pltpu.SMEM((1, K), jnp.int32),
            pltpu.VMEM((1, K), jnp.int32),
            pltpu.SMEM((2,), jnp.int32),
            pltpu.VMEM((BLK, HID), jnp.bfloat16),
            pltpu.VMEM((BLK, HID), jnp.bfloat16),
            pltpu.VMEM((1, K), jnp.float32),
            pltpu.SMEM((1, K), jnp.float32),
            pltpu.SMEM((K,), jnp.int32),
            pltpu.SMEM((K,), jnp.int32),
            pltpu.SMEM((K,), jnp.int32),
            pltpu.VMEM((BLK, HID), jnp.bfloat16),
            pltpu.VMEM((32, 8, BLK), jnp.float32),
            pltpu.VMEM((32, 8, BLK), jnp.float32),
            pltpu.VMEM((16, 8, BLK), jnp.float32),
            pltpu.VMEM((8, BLK), jnp.float32),
            dma((10,)), dma((2,)), dma((5,)), dma((3, 2, 9)), dma((2, 9)), dma((9,)),
            dma((1,)), dma((1,)), dma((5,)), dma((3,)),
        ],
        compiler_params=pltpu.CompilerParams(
            collective_id=0, has_side_effects=True, vmem_limit_bytes=VMEM_BYTES
        ),
    )(features, block_vals, block_cols, block_counts, hub_parts, send_blocks, weight, grad_out)


def solution(mesh):
    placed = (
        P(("nodes", "feat"), None),
        P(("nodes", "feat"), None, None, None),
        P(("nodes", "feat"), None),
        P(("nodes", "feat"), None),
        P(),
        P(("nodes", "feat"), None),
        P(),
        P(("nodes", "feat"), None),
    )
    return jax.shard_map(
        per_device,
        mesh=mesh,
        in_specs=placed,
        out_specs=(P(("nodes", "feat"), None), P()),
        check_vma=False,
    )
```

```python
import math

import jax
import jax.numpy as jnp
from jax import lax
from jax.experimental import pallas as pl
from jax.experimental.pallas import tpu as pltpu
from jax.sharding import PartitionSpec as P

KL, KH, K = 2, 8, 122
BLK, HID = 128, 256
MESH = pl.DeviceIdType.MESH
ALL = slice(None)
A_ROWS = pl.ds(0, 16)
ROWS = (pl.ds(16, 48), pl.ds(64, 64))
HALVES = (pl.ds(0, 2), pl.ds(2, 2))
LAST = 8
A_LAG = 1
ACROSS_LAG = 2
DIRECT = (LAST,)
CHUNK = 61
WORK_STEPS = 8
VMEM_BYTES = 63 << 20


def where_am_i():
    n = lax.axis_index("nodes")
    return n // 8, (n // 2) % 4, n % 2, lax.axis_index("feat")


def device(z, x, c, y):
    return ((z % 16) * 8 + (x % 4) * 2 + c, y % 4)


def kernel(
    feat_hbm, vals_hbm, cols_hbm, counts_hbm, hubs_hbm, send_hbm, weight_hbm, grad_hbm,
    layer_hbm, wgrad_hbm,
    G, S, S_sm, vals, cols, counts_v, hubs, weight, grad_out, frac_v, frac, index, srow, stride,
    layer, W, R1, R2, total_strip,
    local_sem, sent_sem, small_recv, z_recv, one_recv, two_recv, c_recv, s_sent, s_recv, r_recv,
):
    z, x, c, y = where_am_i()
    first = c == 0

    def at_u(d):
        return device(z, x + jnp.where(first, d, 0), c, y + jnp.where(first, 0, d))

    def at_v(d):
        return device(z, x + jnp.where(first, 0, d), c, y + jnp.where(first, d, 0))

    at_uv = (at_u, at_v)
    z_peer = (device(z + 1, x, c, y), device(z + 15, x, c, y))
    other = device(z, x, 1 - c, y)

    barrier = pltpu.get_barrier_semaphore()
    greeted = [device(z, x + d, c, y) for d in (1, 2, 3)]
    greeted += [device(z, x, c, y + d) for d in (1, 2, 3)]
    greeted += [*z_peer, other]
    for peer in greeted:
        pl.semaphore_signal(barrier, inc=1, device_id=peer, device_id_type=MESH)

    def load(i, src, dst):
        copy = pltpu.make_async_copy(src, dst, local_sem.at[i])
        copy.start()
        return copy

    own = G.at[0, 0, 0]
    got_feat = load(0, feat_hbm, own.at[0, 0])
    got_send = load(1, send_hbm, S.at[8, 0, 0])
    got_counts = load(2, counts_hbm, counts_v)
    got_cols = load(3, cols_hbm, cols)
    got_hubs = load(4, hubs_hbm, hubs)
    got_vals = load(5, vals_hbm.at[0], vals)
    got_weight = load(6, weight_hbm, weight)
    got_grad = load(7, grad_hbm, grad_out)
    pl.semaphore_wait(barrier, len(greeted))

    lines = G.reshape(512 * BLK, BLK)
    sent_rows = []

    def wait_rows(sem, rows):
        part = lines.at[pl.ds(0, rows)]
        pltpu.make_async_copy(part, part, sem).wait()

    def send(src, dst, sem, peer, near_core=False):
        rows = math.prod(src.shape[:-1])
        pltpu.make_async_remote_copy(
            src_ref=src, dst_ref=dst, send_sem=sent_sem.at[int(near_core)], recv_sem=sem,
            device_id=peer, device_id_type=MESH,
        ).start()
        if not near_core:
            sent_rows.append(rows)
        return sem, rows

    def arrived(group):
        wait_rows(group[0][0], sum(rows for _, rows in group))

    front = pl.ds(0, 64)
    small_v = {
        d: send(feat_hbm.at[front], own.at[0, d, front], small_recv.at[0 if d == 1 else 1], at_v(d))
        for d in (1, 3, 2)
    }
    small_u = {
        d: send(feat_hbm.at[ROWS[1]], own.at[d, 0, ROWS[1]], small_recv.at[2 if d == 1 else 3], at_u(d))
        for d in (1, 3, 2)
    }
    got_send.wait()
    s_rows = []

    def s_send(i, peer, src, dst):
        pltpu.make_async_remote_copy(
            src_ref=src, dst_ref=dst, send_sem=s_sent.at[0], recv_sem=s_recv.at[i],
            device_id=peer, device_id_type=MESH,
        ).start()
        s_rows.append(math.prod(src.shape[:-2]))
        return i, s_rows[-1]

    def s_wait(sem, rows):
        part = S.reshape(128, 1, BLK).at[pl.ds(0, rows)]
        pltpu.make_async_copy(part, part, sem).wait()

    def s_arrived(group):
        s_wait(s_recv.at[group[0][0]], sum(rows for _, rows in group))

    def s_shift(i, d, low, count):
        src, dst = S.at[pl.ds(8 + low, count)], S.at[pl.ds(8 + low + d, count)]
        return s_send(i, device(z + d + 16, x, c, y), src, dst)

    s_moves = [s_send(0, device(z, x + d, c, y), S.at[8, 0, 0], S.at[8, 0, d]) for d in (1, 3, 2)]

    def strip(p, k, way, place, half=ALL):
        if p == 0:
            return G.at[0, k, way, place, half, ROWS[0]]
        if p == 1:
            return G.at[0, k, way, half, place, ROWS[1]]
        return G.at[0, k, way, half, ALL, A_ROWS]

    def slot(k, way):
        return (0, 1) if k == LAST else (k, way)

    def z_forward(p, k, h):
        copies = []
        for way in (0, 1):
            if k + 1 == LAST and way == (0 if p == 2 else 1):
                continue
            kk, ww = slot(k + 1, way)
            src = strip(p, k, way if k else 0, 0, HALVES[h])
            dst = strip(p, kk, ww, 0, HALVES[h])
            copies.append(send(src, dst, z_recv.at[p, h, k], z_peer[way]))
        return copies

    def pair(k):
        if k == 0:
            return 0, 0
        if k == LAST:
            return 0, 1
        return k, ALL

    def large_one(p, k, h):
        kk, ww = pair(k)
        half = HALVES[h] if k else ALL
        return [
            send(strip(p, kk, ww, 0, half), strip(p, kk, ww, d, half), one_recv.at[p, h, k], at_uv[p](d))
            for d in ((1, 3, 2) if k in DIRECT else (1, 3))
        ]

    def large_two(p, k, h):
        copies = []
        if k in DIRECT:
            return copies
        half = HALVES[h] if k else ALL
        for i, d in enumerate((1, 3)):
            if k == 0 and i == 1 or k == LAST and i == 0:
                continue
            kk = 0 if k == LAST else k
            copies.append(send(strip(p, kk, i, d, half), strip(p, kk, i, 2, half), two_recv.at[k], at_uv[p](d)))
        return copies

    def across(part):
        return [send(G.at[(0, *part)], G.at[(1, *part)], c_recv.at[0], other, True)]

    def rest_across(k):
        kk, ww = pair(k)
        return across((kk, ww, ALL, ALL, pl.ds(16, 112)))

    def a_across(k):
        kk, ww = pair(k)
        return across((kk, ww, ALL, ALL, A_ROWS))

    def base_of(p):
        away = (z - (p >> 3)) & 15
        cell = jnp.where(away < 8, 2 * away, (33 - 2 * away) & 15)
        core = p & 1
        rel = core ^ c
        along = (x - ((p >> 1) & 3)) & 3
        base = (rel * 16 + cell) * 16 + along * jnp.where(core == 0, 4, 1)
        return base, jnp.where(core == 0, 1, 4), ((away + 8) & 15) * 8 + rel * 4 + along

    mine = z * 8 + x * 2 + c

    def near(s, _):
        base, step, _row = base_of(mine)
        index[s] = base + ((y - cols[0, s]) & 3) * step
        return 0

    def hub(s, _):
        v = cols[0, s]
        base, step, _row = base_of(hubs[v >> 2])
        index[s] = base + ((y - v) & 3) * step
        return 0

    def far(s, _):
        base, step, row = base_of(cols[0, s])
        index[s] = base
        stride[s] = step
        srow[s] = row
        return 0

    def resolve(s, _):
        row = srow[s]
        sent = S_sm[row >> 3, (row >> 2) & 1, row & 3, 0, mine]
        index[s] = index[s] + ((y - sent) & 3) * stride[s]
        return 0

    def scale(s, _):
        vals[s] = (frac[0, s] * vals[s].astype(jnp.float32)).astype(jnp.bfloat16)
        return 0

    def portion(body, low, high, part, parts):
        per = (high - low + parts - 1) // parts
        if 0 <= part < parts:
            lax.fori_loop(low + part * per, min(high, low + (part + 1) * per), body, 0)

    z_moves = {}
    ones = {}
    twos = {}
    crossing = []
    got_counts.wait()
    counts = counts_v[...].astype(jnp.float32)
    frac_v[...] = counts / jnp.sum(counts, axis=1, keepdims=True)
    got_frac = load(8, frac_v, frac)
    got_feat.wait()
    arrived([small_v[1]])
    z_moves[0, 0, 1] = z_forward(0, 0, 0)
    arrived([small_u[1]])
    z_moves[1, 0, 1] = z_forward(1, 0, 0)
    arrived([small_v[3], small_v[2]])
    z_moves[0, 1, 1] = z_forward(0, 0, 1)
    ones[0, 0, 0] = large_one(0, 0, 0)
    a_small = [send(own.at[0, ALL, A_ROWS], own.at[d, ALL, A_ROWS], small_recv.at[4], at_u(d)) for d in (1, 3, 2)]
    arrived([small_u[3], small_u[2]])
    z_moves[1, 1, 1] = z_forward(1, 0, 1)
    ones[1, 0, 0] = large_one(1, 0, 0)
    got_cols.wait()
    got_hubs.wait()
    lax.fori_loop(0, KL, near, 0)
    lax.fori_loop(KL, KL + KH, hub, 0)
    s_arrived(s_moves)
    s_moves = [s_send(1, other, S.at[8, 0], S.at[8, 1])]
    got_frac.wait()
    got_vals.wait()
    got_s = None

    def z_step(p, h, k):
        if 1 <= k <= LAST:
            arrived(z_moves[p, h, k])
            if k < LAST:
                z_moves[p, h, k + 1] = z_forward(p, k, h)
            if p < 2:
                ones[p, h, k] = large_one(p, k, h)

    def plane_step(p, h, k):
        if (p, h, k) in ones:
            arrived(ones[p, h, k])
            twos.setdefault(k, []).extend(large_two(p, k, h))

    for k in range(1, LAST + ACROSS_LAG + 1):
        portion(scale, 0, K, k - 1, WORK_STEPS)
        portion(far, KL + KH, K, k - 1, 4)
        portion(resolve, KL + KH, K, k - 9, 2)
        z_step(0, 0, k)
        z_step(1, 0, k)
        plane_step(0, 0, k - 1)
        plane_step(1, 0, k - 1)
        z_step(0, 1, k)
        plane_step(0, 1, k - 1)
        z_step(1, 1, k)
        plane_step(1, 1, k - 1)
        late = k - ACROSS_LAG
        if 0 <= late <= LAST and late not in DIRECT:
            arrived(twos[late])
            crossing += rest_across(late)
        if k - 1 in DIRECT:
            crossing += rest_across(k - 1)
        step = k - A_LAG
        if step == 0:
            arrived(a_small)
            z_moves[2, 0, 1] = z_forward(2, 0, 0)
            z_moves[2, 1, 1] = z_forward(2, 0, 1)
        z_step(2, 0, step)
        z_step(2, 1, step)
        if 0 <= step <= LAST:
            crossing += a_across(step)
        if k == 1:
            s_arrived(s_moves)
            s_moves = [s_shift(2, 1, 0, 1), s_shift(2, -1, 0, 1)]
        if k == 3:
            s_arrived(s_moves)
            s_moves = [s_shift(3, 3, -1, 3), s_shift(3, -3, -1, 3)]
        if k == 5:
            s_arrived(s_moves)
            s_moves = [s_shift(4, 4, 1, 3), s_shift(4, -4, -4, 4)]
        if k == 7:
            s_arrived(s_moves)
            got_s = load(9, S, S_sm)
        if k == 8:
            got_s.wait()

    arrived(crossing)

    flat = G.reshape(512, BLK, BLK)

    def chunk_dot(s, count):
        left = jnp.concatenate([vals[s + i] for i in range(count)], axis=1)
        right = jnp.concatenate([flat[index[s + i]] for i in range(count)], axis=0)
        return jnp.dot(left, right, preferred_element_type=jnp.float32)

    total = lax.fori_loop(1, K // CHUNK, lambda i, acc: acc + chunk_dot(i * CHUNK, CHUNK), chunk_dot(0, CHUNK))
    hidden = total.astype(jnp.bfloat16)
    got_grad.wait()
    grad = lax.dot_general(hidden, grad_out[...], (((0,), (0,)), ((), ())), preferred_element_type=jnp.float32)
    for i in range(16):
        W[i] = grad[8 * i : 8 * i + 8]

    me = x * 4 + y
    owner = c == 1
    plane = sorted(
        ((dx, dy) for dx in range(4) for dy in range(4)),
        key=lambda d: -min(d[0], 4 - d[0]) - min(d[1], 4 - d[1]),
    )

    def at_strip(i):
        return wgrad_hbm.at[pl.ds(pl.multiple_of(8 * i, 8), 8)]

    def strip_send(src, dst, sem, peer):
        pltpu.make_async_remote_copy(
            src_ref=src, dst_ref=dst, send_sem=sent_sem.at[2], recv_sem=sem,
            device_id=peer, device_id_type=MESH,
        ).start()

    def wait_strips(sem, count):
        wait_rows(sem, 32 * count)

    for j, (dx, dy) in enumerate(plane):
        px, py = (x + dx) % 4, (y + dy) % 4

        def scatter(px=px, py=py, j=j):
            strip_send(W.at[px * 4 + py], R1.at[2 * j + c], r_recv.at[0], device(z, px, 1, py))

        if dx or dy:
            scatter()
        else:
            pl.when(c == 0)(scatter)

    @pl.when(owner)
    def _():
        R1[31] = W[me]
        wait_strips(r_recv.at[0], 31)
        R2[0] = jnp.sum(R1[...], axis=0)
        for j in (8, 7, 9, 6, 10, 5, 11, 4, 12, 3, 13, 2, 14, 1, 15):
            strip_send(R2.at[0], R2.at[j], r_recv.at[1], device(z + j, x, c, y))

    got_weight.wait()
    layer[...] = jnp.dot(hidden, weight[...], preferred_element_type=jnp.float32).astype(jnp.bfloat16)
    put_layer = load(0, layer, layer_hbm)
    s_wait(s_sent.at[0], sum(s_rows))
    wait_rows(sent_sem.at[0], sum(sent_rows))
    wait_rows(sent_sem.at[1], sum(rows for _, rows in crossing))
    put_layer.wait()

    @pl.when(owner)
    def _():
        wait_strips(r_recv.at[1], 15)
        total_strip[...] = jnp.sum(R2[...], axis=0)
        for dx, dy in plane:
            px, py = (x + dx) % 4, (y + dy) % 4
            strip_send(total_strip, at_strip(me), r_recv.at[2], device(z, px, 0, py))
            if dx or dy:
                strip_send(total_strip, at_strip(me), r_recv.at[2], device(z, px, 1, py))
        put_strip = load(1, total_strip, at_strip(me))
        put_strip.wait()
        wait_strips(r_recv.at[2], 15)
        wait_strips(sent_sem.at[2], 15 + 15 + 31)

    @pl.when(c == 0)
    def _():
        wait_strips(r_recv.at[2], 16)
        wait_strips(sent_sem.at[2], 16)


def hand_over(layer_from, wgrad_from, layer_to, wgrad_to, layer, wgrad, sem):
    fetch = [
        pltpu.make_async_copy(layer_from, layer, sem.at[0]),
        pltpu.make_async_copy(wgrad_from, wgrad, sem.at[1]),
    ]
    store = [
        pltpu.make_async_copy(layer, layer_to, sem.at[2]),
        pltpu.make_async_copy(wgrad, wgrad_to, sem.at[3]),
    ]
    for copy in fetch:
        copy.start()
    for copy, then in zip(fetch, store):
        copy.wait()
        then.start()
    for copy in store:
        copy.wait()


def per_device(features, block_vals, block_cols, block_counts, hub_parts, send_blocks, weight, grad_out):
    dma = pltpu.SemaphoreType.DMA
    anywhere = pl.BlockSpec(memory_space=pl.ANY)
    outs = (
        jax.ShapeDtypeStruct((BLK, HID), jnp.bfloat16),
        jax.ShapeDtypeStruct((BLK, HID), jnp.float32),
    )
    results = pl.pallas_call(
        kernel,
        out_shape=outs,
        in_specs=[anywhere] * 8,
        out_specs=(anywhere,) * 2,
        scratch_shapes=[
            pltpu.VMEM((2, 8, 2, 4, 4, BLK, BLK), jnp.bfloat16),
            pltpu.VMEM((16, 2, 4, 1, BLK), jnp.int32),
            pltpu.SMEM((16, 2, 4, 1, BLK), jnp.int32),
            pltpu.VMEM((K, BLK, BLK), jnp.bfloat16),
            pltpu.SMEM((1, K), jnp.int32),
            pltpu.VMEM((1, K), jnp.int32),
            pltpu.SMEM((2,), jnp.int32),
            pltpu.VMEM((BLK, HID), jnp.bfloat16),
            pltpu.VMEM((BLK, HID), jnp.bfloat16),
            pltpu.VMEM((1, K), jnp.float32),
            pltpu.SMEM((1, K), jnp.float32),
            pltpu.SMEM((K,), jnp.int32),
            pltpu.SMEM((K,), jnp.int32),
            pltpu.SMEM((K,), jnp.int32),
            pltpu.VMEM((BLK, HID), jnp.bfloat16),
            pltpu.VMEM((16, 8, HID), jnp.float32),
            pltpu.VMEM((32, 8, HID), jnp.float32),
            pltpu.VMEM((16, 8, HID), jnp.float32),
            pltpu.VMEM((8, HID), jnp.float32),
            dma((10,)), dma((3,)), dma((5,)), dma((3, 2, 9)), dma((2, 2, 9)), dma((9,)),
            dma((1,)), dma((1,)), dma((5,)), dma((3,)),
        ],
        compiler_params=pltpu.CompilerParams(
            collective_id=0, has_side_effects=True, vmem_limit_bytes=VMEM_BYTES
        ),
    )(features, block_vals, block_cols, block_counts, hub_parts, send_blocks, weight, grad_out)
    return pl.pallas_call(
        hand_over,
        out_shape=outs,
        in_specs=[anywhere] * 2,
        out_specs=(anywhere,) * 2,
        scratch_shapes=[pltpu.VMEM((BLK, HID), jnp.bfloat16), pltpu.VMEM((BLK, HID), jnp.float32), dma((4,))],
        compiler_params=pltpu.CompilerParams(vmem_limit_bytes=VMEM_BYTES),
    )(*results)


def solution(mesh):
    placed = (
        P(("nodes", "feat"), None),
        P(("nodes", "feat"), None, None, None),
        P(("nodes", "feat"), None),
        P(("nodes", "feat"), None),
        P(),
        P(("nodes", "feat"), None),
        P(),
        P(("nodes", "feat"), None),
    )
    return jax.shard_map(
        per_device,
        mesh=mesh,
        in_specs=placed,
        out_specs=(P(("nodes", "feat"), None), P()),
        check_vma=False,
    )
```

```python
import math

import jax
import jax.numpy as jnp
from jax import lax
from jax.experimental import pallas as pl
from jax.experimental.pallas import tpu as pltpu
from jax.sharding import PartitionSpec as P

KL, KH, K = 2, 8, 122
BLK, HID = 128, 256
MESH = pl.DeviceIdType.MESH
ALL = slice(None)
A_ROWS = pl.ds(0, 16)
ROWS = (pl.ds(16, 48), pl.ds(64, 64))
HALVES = (pl.ds(0, 2), pl.ds(2, 2))
LAST = 8
A_LAG = 1
ACROSS_LAG = 2
DIRECT = (LAST,)
SPLIT = (LAST - 1,)
CHUNK = 61
WORK_STEPS = 6
VMEM_BYTES = 63 << 20


def where_am_i():
    n = lax.axis_index("nodes")
    return n // 8, (n // 2) % 4, n % 2, lax.axis_index("feat")


def device(z, x, c, y):
    return ((z % 16) * 8 + (x % 4) * 2 + c, y % 4)


def kernel(
    feat_hbm, vals_hbm, cols_hbm, counts_hbm, hubs_hbm, send_hbm, weight_hbm, grad_hbm,
    layer_hbm, wgrad_hbm,
    G, S, S_sm, vals, cols, counts_v, hubs, weight, grad_out, frac_v, frac, index, srow, stride,
    layer, W, R1, R2, total_strip,
    local_sem, sent_sem, small_recv, z_recv, one_recv, two_recv, c_recv, s_sent, s_recv, r_recv,
):
    z, x, c, y = where_am_i()
    first = c == 0

    def at_u(d):
        return device(z, x + jnp.where(first, d, 0), c, y + jnp.where(first, 0, d))

    def at_v(d):
        return device(z, x + jnp.where(first, 0, d), c, y + jnp.where(first, d, 0))

    at_uv = (at_u, at_v)
    z_peer = (device(z + 1, x, c, y), device(z + 15, x, c, y))
    other = device(z, x, 1 - c, y)

    barrier = pltpu.get_barrier_semaphore()
    greeted = [device(z, x + d, c, y) for d in (1, 2, 3)]
    greeted += [device(z, x, c, y + d) for d in (1, 2, 3)]
    greeted += [*z_peer, other]
    for peer in greeted:
        pl.semaphore_signal(barrier, inc=1, device_id=peer, device_id_type=MESH)

    def load(i, src, dst):
        copy = pltpu.make_async_copy(src, dst, local_sem.at[i])
        copy.start()
        return copy

    own = G.at[0, 0, 0]
    got_feat = load(0, feat_hbm, own.at[0, 0])
    got_send = load(1, send_hbm, S.at[8, 0, 0])
    got_counts = load(2, counts_hbm, counts_v)
    got_cols = load(3, cols_hbm, cols)
    got_hubs = load(4, hubs_hbm, hubs)
    got_vals = load(5, vals_hbm.at[0], vals)
    got_weight = load(6, weight_hbm, weight)
    got_grad = load(7, grad_hbm, grad_out)
    pl.semaphore_wait(barrier, len(greeted))

    lines = G.reshape(512 * BLK, BLK)
    sent_rows = []

    def wait_rows(sem, rows):
        part = lines.at[pl.ds(0, rows)]
        pltpu.make_async_copy(part, part, sem).wait()

    def send(src, dst, sem, peer, near_core=False):
        rows = math.prod(src.shape[:-1])
        pltpu.make_async_remote_copy(
            src_ref=src, dst_ref=dst, send_sem=sent_sem.at[int(near_core)], recv_sem=sem,
            device_id=peer, device_id_type=MESH,
        ).start()
        if not near_core:
            sent_rows.append(rows)
        return sem, rows

    def arrived(group):
        wait_rows(group[0][0], sum(rows for _, rows in group))

    front = pl.ds(0, 64)
    small_v = {
        d: send(feat_hbm.at[front], own.at[0, d, front], small_recv.at[0 if d == 1 else 1], at_v(d))
        for d in (1, 3, 2)
    }
    small_u = {
        d: send(feat_hbm.at[ROWS[1]], own.at[d, 0, ROWS[1]], small_recv.at[2 if d == 1 else 3], at_u(d))
        for d in (1, 3, 2)
    }
    got_send.wait()
    s_rows = []

    def s_send(i, peer, src, dst):
        pltpu.make_async_remote_copy(
            src_ref=src, dst_ref=dst, send_sem=s_sent.at[0], recv_sem=s_recv.at[i],
            device_id=peer, device_id_type=MESH,
        ).start()
        s_rows.append(math.prod(src.shape[:-2]))
        return i, s_rows[-1]

    def s_wait(sem, rows):
        part = S.reshape(128, 1, BLK).at[pl.ds(0, rows)]
        pltpu.make_async_copy(part, part, sem).wait()

    def s_arrived(group):
        s_wait(s_recv.at[group[0][0]], sum(rows for _, rows in group))

    def s_shift(i, d, low, count):
        src, dst = S.at[pl.ds(8 + low, count)], S.at[pl.ds(8 + low + d, count)]
        return s_send(i, device(z + d + 16, x, c, y), src, dst)

    s_moves = [s_send(0, device(z, x + d, c, y), S.at[8, 0, 0], S.at[8, 0, d]) for d in (1, 3, 2)]

    def strip(p, k, way, place, half=ALL):
        if p == 0:
            return G.at[0, k, way, place, half, ROWS[0]]
        if p == 1:
            return G.at[0, k, way, half, place, ROWS[1]]
        return G.at[0, k, way, half, ALL, A_ROWS]

    def slot(k, way):
        return (0, 1) if k == LAST else (k, way)

    def z_forward(p, k, h):
        copies = []
        for way in (0, 1):
            if k + 1 == LAST and way == (0 if p == 2 else 1):
                continue
            kk, ww = slot(k + 1, way)
            src = strip(p, k, way if k else 0, 0, HALVES[h])
            dst = strip(p, kk, ww, 0, HALVES[h])
            copies.append(send(src, dst, z_recv.at[p, h, k], z_peer[way]))
        return copies

    def pair(k):
        if k == 0:
            return 0, 0
        if k == LAST:
            return 0, 1
        return k, ALL

    def large_one(p, k, h):
        kk, ww = pair(k)
        half = HALVES[h] if k else ALL
        return [
            send(strip(p, kk, ww, 0, half), strip(p, kk, ww, d, half), one_recv.at[p, h, k], at_uv[p](d))
            for d in ((1, 3, 2) if k in DIRECT else (1, 3))
        ]

    def large_two(p, k, h):
        copies = []
        if k in DIRECT:
            return copies
        half = HALVES[h] if k else ALL
        for i, d in enumerate((1, 3)):
            if k == 0 and i == 1 or k == LAST and i == 0:
                continue
            kk = 0 if k == LAST else k
            copies.append(send(strip(p, kk, i, d, half), strip(p, kk, i, 2, half), two_recv.at[k], at_uv[p](d)))
        return copies

    def across(part):
        return [send(G.at[(0, *part)], G.at[(1, *part)], c_recv.at[0], other, True)]

    def places_across(k, *places):
        kk, ww = pair(k)
        copies = []
        for place in places:
            copies += across((kk, ww, place, ALL, ROWS[0])) + across((kk, ww, ALL, place, ROWS[1]))
        return copies

    def last_across(p, h):
        if p == 0:
            return across((0, 1, ALL, HALVES[h], ROWS[0]))
        return across((0, 1, HALVES[h], ALL, ROWS[1]))

    def rest_across(k):
        if k in SPLIT:
            return places_across(k, 2)
        kk, ww = pair(k)
        return across((kk, ww, ALL, ALL, pl.ds(16, 112)))

    def a_across(k):
        kk, ww = pair(k)
        return across((kk, ww, ALL, ALL, A_ROWS))

    def base_of(p):
        away = (z - (p >> 3)) & 15
        cell = jnp.where(away < 8, 2 * away, (33 - 2 * away) & 15)
        core = p & 1
        rel = core ^ c
        along = (x - ((p >> 1) & 3)) & 3
        base = (rel * 16 + cell) * 16 + along * jnp.where(core == 0, 4, 1)
        return base, jnp.where(core == 0, 1, 4), ((away + 8) & 15) * 8 + rel * 4 + along

    mine = z * 8 + x * 2 + c

    def near(s, _):
        base, step, _row = base_of(mine)
        index[s] = base + ((y - cols[0, s]) & 3) * step
        return 0

    def hub(s, _):
        v = cols[0, s]
        base, step, _row = base_of(hubs[v >> 2])
        index[s] = base + ((y - v) & 3) * step
        return 0

    def far(s, _):
        base, step, row = base_of(cols[0, s])
        index[s] = base
        stride[s] = step
        srow[s] = row
        return 0

    def resolve(s, _):
        row = srow[s]
        sent = S_sm[row >> 3, (row >> 2) & 1, row & 3, 0, mine]
        index[s] = index[s] + ((y - sent) & 3) * stride[s]
        return 0

    def scale(s, _):
        vals[s] = (frac[0, s] * vals[s].astype(jnp.float32)).astype(jnp.bfloat16)
        return 0

    def portion(body, low, high, part, parts):
        per = (high - low + parts - 1) // parts
        if 0 <= part < parts:
            lax.fori_loop(low + part * per, min(high, low + (part + 1) * per), body, 0)

    z_moves = {}
    ones = {}
    twos = {}
    crossing = []
    got_counts.wait()
    counts = counts_v[...].astype(jnp.float32)
    frac_v[...] = counts / jnp.sum(counts, axis=1, keepdims=True)
    got_frac = load(8, frac_v, frac)
    got_feat.wait()
    arrived([small_v[1]])
    z_moves[0, 0, 1] = z_forward(0, 0, 0)
    arrived([small_u[1]])
    z_moves[1, 0, 1] = z_forward(1, 0, 0)
    arrived([small_v[3], small_v[2]])
    z_moves[0, 1, 1] = z_forward(0, 0, 1)
    ones[0, 0, 0] = large_one(0, 0, 0)
    a_small = [send(own.at[0, ALL, A_ROWS], own.at[d, ALL, A_ROWS], small_recv.at[4], at_u(d)) for d in (1, 3, 2)]
    arrived([small_u[3], small_u[2]])
    z_moves[1, 1, 1] = z_forward(1, 0, 1)
    ones[1, 0, 0] = large_one(1, 0, 0)
    s_arrived(s_moves)
    s_moves = [s_send(1, other, S.at[8, 0], S.at[8, 1])]
    got_s = None

    def z_step(p, h, k):
        if 1 <= k <= LAST:
            arrived(z_moves[p, h, k])
            if k < LAST:
                z_moves[p, h, k + 1] = z_forward(p, k, h)
            if p < 2:
                ones[p, h, k] = large_one(p, k, h)

    def plane_step(p, h, k):
        if (p, h, k) in ones:
            arrived(ones[p, h, k])
            twos.setdefault(k, []).extend(large_two(p, k, h))
            if k == LAST:
                crossing.extend(last_across(p, h))

    for k in range(1, LAST + ACROSS_LAG + 1):
        if k == 3:
            got_cols.wait()
            got_hubs.wait()
            got_frac.wait()
            got_vals.wait()
            lax.fori_loop(0, KL, near, 0)
            lax.fori_loop(KL, KL + KH, hub, 0)
        portion(scale, 0, K, k - 3, WORK_STEPS)
        portion(far, KL + KH, K, k - 4, 4)
        portion(resolve, KL + KH, K, k - 9, 2)
        z_step(0, 0, k)
        z_step(1, 0, k)
        plane_step(0, 0, k - 1)
        plane_step(1, 0, k - 1)
        z_step(0, 1, k)
        plane_step(0, 1, k - 1)
        z_step(1, 1, k)
        plane_step(1, 1, k - 1)
        late = k - ACROSS_LAG
        if 0 <= late <= LAST and late not in DIRECT:
            arrived(twos[late])
            crossing += rest_across(late)
        if k - 1 in SPLIT:
            crossing += places_across(k - 1, pl.ds(0, 2), 3)
        step = k - A_LAG
        if step == 0:
            arrived(a_small)
            z_moves[2, 0, 1] = z_forward(2, 0, 0)
            z_moves[2, 1, 1] = z_forward(2, 0, 1)
        z_step(2, 0, step)
        z_step(2, 1, step)
        if 0 <= step <= LAST:
            crossing += a_across(step)
        if k == 1:
            s_arrived(s_moves)
            s_moves = [s_shift(2, 1, 0, 1), s_shift(2, -1, 0, 1)]
        if k == 3:
            s_arrived(s_moves)
            s_moves = [s_shift(3, 3, -1, 3), s_shift(3, -3, -1, 3)]
        if k == 5:
            s_arrived(s_moves)
            s_moves = [s_shift(4, 4, 1, 3), s_shift(4, -4, -4, 4)]
        if k == 7:
            s_arrived(s_moves)
            got_s = load(9, S, S_sm)
        if k == 8:
            got_s.wait()

    arrived(crossing)

    flat = G.reshape(512, BLK, BLK)

    def chunk_dot(s, count):
        left = jnp.concatenate([vals[s + i] for i in range(count)], axis=1)
        right = jnp.concatenate([flat[index[s + i]] for i in range(count)], axis=0)
        return jnp.dot(left, right, preferred_element_type=jnp.float32)

    total = lax.fori_loop(1, K // CHUNK, lambda i, acc: acc + chunk_dot(i * CHUNK, CHUNK), chunk_dot(0, CHUNK))
    hidden = total.astype(jnp.bfloat16)
    got_grad.wait()
    grad = lax.dot_general(hidden, grad_out[...], (((0,), (0,)), ((), ())), preferred_element_type=jnp.float32)
    for i in range(16):
        W[i] = grad[8 * i : 8 * i + 8]

    me = x * 4 + y
    owner = c == 1
    plane = sorted(
        ((dx, dy) for dx in range(4) for dy in range(4)),
        key=lambda d: -min(d[0], 4 - d[0]) - min(d[1], 4 - d[1]),
    )

    def at_strip(i):
        return wgrad_hbm.at[pl.ds(pl.multiple_of(8 * i, 8), 8)]

    def strip_send(src, dst, sem, peer):
        pltpu.make_async_remote_copy(
            src_ref=src, dst_ref=dst, send_sem=sent_sem.at[2], recv_sem=sem,
            device_id=peer, device_id_type=MESH,
        ).start()

    def wait_strips(sem, count):
        wait_rows(sem, 32 * count)

    for j, (dx, dy) in enumerate(plane):
        px, py = (x + dx) % 4, (y + dy) % 4

        def scatter(px=px, py=py, j=j):
            strip_send(W.at[px * 4 + py], R1.at[2 * j + c], r_recv.at[0], device(z, px, 1, py))

        if dx or dy:
            scatter()
        else:
            pl.when(c == 0)(scatter)

    @pl.when(owner)
    def _():
        R1[31] = W[me]
        wait_strips(r_recv.at[0], 31)
        R2[0] = jnp.sum(R1[...], axis=0)
        for j in (8, 7, 9, 6, 10, 5, 11, 4, 12, 3, 13, 2, 14, 1, 15):
            strip_send(R2.at[0], R2.at[j], r_recv.at[1], device(z + j, x, c, y))

    got_weight.wait()
    layer[...] = jnp.dot(hidden, weight[...], preferred_element_type=jnp.float32).astype(jnp.bfloat16)
    put_layer = load(0, layer, layer_hbm)
    s_wait(s_sent.at[0], sum(s_rows))
    wait_rows(sent_sem.at[0], sum(sent_rows))
    wait_rows(sent_sem.at[1], sum(rows for _, rows in crossing))
    put_layer.wait()

    @pl.when(owner)
    def _():
        wait_strips(r_recv.at[1], 15)
        total_strip[...] = jnp.sum(R2[...], axis=0)
        for dx, dy in plane:
            px, py = (x + dx) % 4, (y + dy) % 4
            strip_send(total_strip, at_strip(me), r_recv.at[2], device(z, px, 0, py))
            if dx or dy:
                strip_send(total_strip, at_strip(me), r_recv.at[2], device(z, px, 1, py))
        put_strip = load(1, total_strip, at_strip(me))
        put_strip.wait()
        wait_strips(r_recv.at[2], 15)
        wait_strips(sent_sem.at[2], 15 + 15 + 31)

    @pl.when(c == 0)
    def _():
        wait_strips(r_recv.at[2], 16)
        wait_strips(sent_sem.at[2], 16)


def hand_over(layer_from, wgrad_from, layer_to, wgrad_to, layer, wgrad, sem):
    fetch = [
        pltpu.make_async_copy(layer_from, layer, sem.at[0]),
        pltpu.make_async_copy(wgrad_from, wgrad, sem.at[1]),
    ]
    store = [
        pltpu.make_async_copy(layer, layer_to, sem.at[2]),
        pltpu.make_async_copy(wgrad, wgrad_to, sem.at[3]),
    ]
    for copy in fetch:
        copy.start()
    for copy, then in zip(fetch, store):
        copy.wait()
        then.start()
    for copy in store:
        copy.wait()


def per_device(features, block_vals, block_cols, block_counts, hub_parts, send_blocks, weight, grad_out):
    dma = pltpu.SemaphoreType.DMA
    anywhere = pl.BlockSpec(memory_space=pl.ANY)
    outs = (
        jax.ShapeDtypeStruct((BLK, HID), jnp.bfloat16),
        jax.ShapeDtypeStruct((BLK, HID), jnp.float32),
    )
    results = pl.pallas_call(
        kernel,
        out_shape=outs,
        in_specs=[anywhere] * 8,
        out_specs=(anywhere,) * 2,
        scratch_shapes=[
            pltpu.VMEM((2, 8, 2, 4, 4, BLK, BLK), jnp.bfloat16),
            pltpu.VMEM((16, 2, 4, 1, BLK), jnp.int32),
            pltpu.SMEM((16, 2, 4, 1, BLK), jnp.int32),
            pltpu.VMEM((K, BLK, BLK), jnp.bfloat16),
            pltpu.SMEM((1, K), jnp.int32),
            pltpu.VMEM((1, K), jnp.int32),
            pltpu.SMEM((2,), jnp.int32),
            pltpu.VMEM((BLK, HID), jnp.bfloat16),
            pltpu.VMEM((BLK, HID), jnp.bfloat16),
            pltpu.VMEM((1, K), jnp.float32),
            pltpu.SMEM((1, K), jnp.float32),
            pltpu.SMEM((K,), jnp.int32),
            pltpu.SMEM((K,), jnp.int32),
            pltpu.SMEM((K,), jnp.int32),
            pltpu.VMEM((BLK, HID), jnp.bfloat16),
            pltpu.VMEM((16, 8, HID), jnp.float32),
            pltpu.VMEM((32, 8, HID), jnp.float32),
            pltpu.VMEM((16, 8, HID), jnp.float32),
            pltpu.VMEM((8, HID), jnp.float32),
            dma((10,)), dma((3,)), dma((5,)), dma((3, 2, 9)), dma((2, 2, 9)), dma((9,)),
            dma((1,)), dma((1,)), dma((5,)), dma((3,)),
        ],
        compiler_params=pltpu.CompilerParams(
            collective_id=0, has_side_effects=True, vmem_limit_bytes=VMEM_BYTES
        ),
    )(features, block_vals, block_cols, block_counts, hub_parts, send_blocks, weight, grad_out)
    return pl.pallas_call(
        hand_over,
        out_shape=outs,
        in_specs=[anywhere] * 2,
        out_specs=(anywhere,) * 2,
        scratch_shapes=[pltpu.VMEM((BLK, HID), jnp.bfloat16), pltpu.VMEM((BLK, HID), jnp.float32), dma((4,))],
        compiler_params=pltpu.CompilerParams(vmem_limit_bytes=VMEM_BYTES),
    )(*results)


def solution(mesh):
    placed = (
        P(("nodes", "feat"), None),
        P(("nodes", "feat"), None, None, None),
        P(("nodes", "feat"), None),
        P(("nodes", "feat"), None),
        P(),
        P(("nodes", "feat"), None),
        P(),
        P(("nodes", "feat"), None),
    )
    return jax.shard_map(
        per_device,
        mesh=mesh,
        in_specs=placed,
        out_specs=(P(("nodes", "feat"), None), P()),
        check_vma=False,
    )
```

```python
import math

import jax
import jax.numpy as jnp
from jax import lax
from jax.experimental import pallas as pl
from jax.experimental.pallas import tpu as pltpu
from jax.sharding import PartitionSpec as P

KL, KH, K = 2, 8, 122
BLK, HID = 128, 256
MESH = pl.DeviceIdType.MESH
ALL = slice(None)
A_ROWS = pl.ds(0, 16)
ROWS = (pl.ds(16, 48), pl.ds(64, 64))
HALVES = (pl.ds(0, 2), pl.ds(2, 2))
LAST = 8
A_LAG = 1
ACROSS_LAG = 2
DIRECT = (LAST,)
SPLIT = (LAST - 1,)
CHUNK = K
WORK_STEPS = 6
VMEM_BYTES = 63 << 20


def where_am_i():
    n = lax.axis_index("nodes")
    return n // 8, (n // 2) % 4, n % 2, lax.axis_index("feat")


def device(z, x, c, y):
    return ((z % 16) * 8 + (x % 4) * 2 + c, y % 4)


def kernel(
    feat_hbm, vals_hbm, cols_hbm, counts_hbm, hubs_hbm, send_hbm, weight_hbm, grad_hbm,
    layer_hbm, wgrad_hbm,
    G, S, S_sm, vals, cols, counts_v, hubs, weight, grad_out, frac_v, frac, index, srow, stride,
    layer, W, R1, R2, total_strip,
    local_sem, sent_sem, small_recv, z_recv, one_recv, two_recv, c_recv, s_sent, s_recv, r_recv,
):
    z, x, c, y = where_am_i()
    first = c == 0

    def at_u(d):
        return device(z, x + jnp.where(first, d, 0), c, y + jnp.where(first, 0, d))

    def at_v(d):
        return device(z, x + jnp.where(first, 0, d), c, y + jnp.where(first, d, 0))

    at_uv = (at_u, at_v)
    z_peer = (device(z + 1, x, c, y), device(z + 15, x, c, y))
    other = device(z, x, 1 - c, y)

    barrier = pltpu.get_barrier_semaphore()
    greeted = [device(z, x + d, c, y) for d in (1, 2, 3)]
    greeted += [device(z, x, c, y + d) for d in (1, 2, 3)]
    greeted += [*z_peer, other]
    for peer in greeted:
        pl.semaphore_signal(barrier, inc=1, device_id=peer, device_id_type=MESH)

    def load(i, src, dst):
        copy = pltpu.make_async_copy(src, dst, local_sem.at[i])
        copy.start()
        return copy

    own = G.at[0, 0, 0]
    got_feat = load(0, feat_hbm, own.at[0, 0])
    got_send = load(1, send_hbm, S.at[8, 0, 0])
    got_counts = load(2, counts_hbm, counts_v)
    got_cols = load(3, cols_hbm, cols)
    got_hubs = load(4, hubs_hbm, hubs)
    got_vals = load(5, vals_hbm.at[0], vals)
    got_weight = load(6, weight_hbm, weight)
    got_grad = load(7, grad_hbm, grad_out)
    pl.semaphore_wait(barrier, len(greeted))

    lines = G.reshape(512 * BLK, BLK)
    sent_rows = []

    def wait_rows(sem, rows):
        part = lines.at[pl.ds(0, rows)]
        pltpu.make_async_copy(part, part, sem).wait()

    def send(src, dst, sem, peer, near_core=False):
        rows = math.prod(src.shape[:-1])
        pltpu.make_async_remote_copy(
            src_ref=src, dst_ref=dst, send_sem=sent_sem.at[int(near_core)], recv_sem=sem,
            device_id=peer, device_id_type=MESH,
        ).start()
        if not near_core:
            sent_rows.append(rows)
        return sem, rows

    def arrived(group):
        wait_rows(group[0][0], sum(rows for _, rows in group))

    front = pl.ds(0, 64)
    small_v = {
        d: send(feat_hbm.at[front], own.at[0, d, front], small_recv.at[0 if d == 1 else 1], at_v(d))
        for d in (1, 3, 2)
    }
    small_u = {
        d: send(feat_hbm.at[ROWS[1]], own.at[d, 0, ROWS[1]], small_recv.at[2 if d == 1 else 3], at_u(d))
        for d in (1, 3, 2)
    }
    got_send.wait()
    s_rows = []

    def s_send(i, peer, src, dst):
        pltpu.make_async_remote_copy(
            src_ref=src, dst_ref=dst, send_sem=s_sent.at[0], recv_sem=s_recv.at[i],
            device_id=peer, device_id_type=MESH,
        ).start()
        s_rows.append(math.prod(src.shape[:-2]))
        return i, s_rows[-1]

    def s_wait(sem, rows):
        part = S.reshape(128, 1, BLK).at[pl.ds(0, rows)]
        pltpu.make_async_copy(part, part, sem).wait()

    def s_arrived(group):
        s_wait(s_recv.at[group[0][0]], sum(rows for _, rows in group))

    def s_shift(i, d, low, count):
        src, dst = S.at[pl.ds(8 + low, count)], S.at[pl.ds(8 + low + d, count)]
        return s_send(i, device(z + d + 16, x, c, y), src, dst)

    s_moves = [s_send(0, device(z, x + d, c, y), S.at[8, 0, 0], S.at[8, 0, d]) for d in (1, 3, 2)]

    def strip(p, k, way, place, half=ALL):
        if p == 0:
            return G.at[0, k, way, place, half, ROWS[0]]
        if p == 1:
            return G.at[0, k, way, half, place, ROWS[1]]
        return G.at[0, k, way, half, ALL, A_ROWS]

    def slot(k, way):
        return (0, 1) if k == LAST else (k, way)

    def z_forward(p, k, h):
        copies = []
        for way in (0, 1):
            if k + 1 == LAST and way == (0 if p == 2 else 1):
                continue
            kk, ww = slot(k + 1, way)
            src = strip(p, k, way if k else 0, 0, HALVES[h])
            dst = strip(p, kk, ww, 0, HALVES[h])
            copies.append(send(src, dst, z_recv.at[p, h, k], z_peer[way]))
        return copies

    def pair(k):
        if k == 0:
            return 0, 0
        if k == LAST:
            return 0, 1
        return k, ALL

    def large_one(p, k, h):
        kk, ww = pair(k)
        half = HALVES[h] if k else ALL
        return [
            send(strip(p, kk, ww, 0, half), strip(p, kk, ww, d, half), one_recv.at[p, h, k], at_uv[p](d))
            for d in ((1, 3, 2) if k in DIRECT else (1, 3))
        ]

    def large_two(p, k, h):
        copies = []
        if k in DIRECT:
            return copies
        half = HALVES[h] if k else ALL
        for i, d in enumerate((1, 3)):
            if k == 0 and i == 1 or k == LAST and i == 0:
                continue
            kk = 0 if k == LAST else k
            copies.append(send(strip(p, kk, i, d, half), strip(p, kk, i, 2, half), two_recv.at[k], at_uv[p](d)))
        return copies

    def across(part):
        return [send(G.at[(0, *part)], G.at[(1, *part)], c_recv.at[0], other, True)]

    def places_across(k, *places):
        kk, ww = pair(k)
        copies = []
        for place in places:
            copies += across((kk, ww, place, ALL, ROWS[0])) + across((kk, ww, ALL, place, ROWS[1]))
        return copies

    def last_across(p, h):
        if p == 0:
            return across((0, 1, ALL, HALVES[h], ROWS[0]))
        return across((0, 1, HALVES[h], ALL, ROWS[1]))

    def rest_across(k):
        if k in SPLIT:
            return places_across(k, 2)
        kk, ww = pair(k)
        return across((kk, ww, ALL, ALL, pl.ds(16, 112)))

    def a_across(k):
        kk, ww = pair(k)
        return across((kk, ww, ALL, ALL, A_ROWS))

    def base_of(p):
        away = (z - (p >> 3)) & 15
        cell = jnp.where(away < 8, 2 * away, (33 - 2 * away) & 15)
        core = p & 1
        rel = core ^ c
        along = (x - ((p >> 1) & 3)) & 3
        base = (rel * 16 + cell) * 16 + along * jnp.where(core == 0, 4, 1)
        return base, jnp.where(core == 0, 1, 4), ((away + 8) & 15) * 8 + rel * 4 + along

    mine = z * 8 + x * 2 + c

    def near(s, _):
        base, step, _row = base_of(mine)
        index[s] = base + ((y - cols[0, s]) & 3) * step
        return 0

    def hub(s, _):
        v = cols[0, s]
        base, step, _row = base_of(hubs[v >> 2])
        index[s] = base + ((y - v) & 3) * step
        return 0

    def far(s, _):
        base, step, row = base_of(cols[0, s])
        index[s] = base
        stride[s] = step
        srow[s] = row
        return 0

    def resolve(s, _):
        row = srow[s]
        sent = S_sm[row >> 3, (row >> 2) & 1, row & 3, 0, mine]
        index[s] = index[s] + ((y - sent) & 3) * stride[s]
        return 0

    def scale(s, _):
        vals[s] = (frac[0, s] * vals[s].astype(jnp.float32)).astype(jnp.bfloat16)
        return 0

    def portion(body, low, high, part, parts):
        per = (high - low + parts - 1) // parts
        if 0 <= part < parts:
            lax.fori_loop(low + part * per, min(high, low + (part + 1) * per), body, 0)

    z_moves = {}
    ones = {}
    twos = {}
    crossing = []
    got_counts.wait()
    counts = counts_v[...].astype(jnp.float32)
    frac_v[...] = counts / jnp.sum(counts, axis=1, keepdims=True)
    got_frac = load(8, frac_v, frac)
    got_feat.wait()
    arrived([small_v[1]])
    z_moves[0, 0, 1] = z_forward(0, 0, 0)
    arrived([small_u[1]])
    z_moves[1, 0, 1] = z_forward(1, 0, 0)
    arrived([small_v[3], small_v[2]])
    z_moves[0, 1, 1] = z_forward(0, 0, 1)
    ones[0, 0, 0] = large_one(0, 0, 0)
    a_small = [send(own.at[0, ALL, A_ROWS], own.at[d, ALL, A_ROWS], small_recv.at[4], at_u(d)) for d in (1, 3, 2)]
    arrived([small_u[3], small_u[2]])
    z_moves[1, 1, 1] = z_forward(1, 0, 1)
    ones[1, 0, 0] = large_one(1, 0, 0)
    s_arrived(s_moves)
    s_moves = [s_send(1, other, S.at[8, 0], S.at[8, 1])]
    got_s = None

    def z_step(p, h, k):
        if 1 <= k <= LAST:
            arrived(z_moves[p, h, k])
            if k < LAST:
                z_moves[p, h, k + 1] = z_forward(p, k, h)
            if p < 2:
                ones[p, h, k] = large_one(p, k, h)

    def plane_step(p, h, k):
        if (p, h, k) in ones:
            arrived(ones[p, h, k])
            twos.setdefault(k, []).extend(large_two(p, k, h))
            if k == LAST:
                crossing.extend(last_across(p, h))

    for k in range(1, LAST + ACROSS_LAG + 1):
        if k == 3:
            got_cols.wait()
            got_hubs.wait()
            got_frac.wait()
            got_vals.wait()
            lax.fori_loop(0, KL, near, 0)
            lax.fori_loop(KL, KL + KH, hub, 0)
        portion(scale, 0, K, k - 3, WORK_STEPS)
        portion(far, KL + KH, K, k - 4, 4)
        portion(resolve, KL + KH, K, k - 9, 2)
        z_step(0, 0, k)
        z_step(1, 0, k)
        plane_step(0, 0, k - 1)
        plane_step(1, 0, k - 1)
        z_step(0, 1, k)
        plane_step(0, 1, k - 1)
        z_step(1, 1, k)
        plane_step(1, 1, k - 1)
        late = k - ACROSS_LAG
        if 0 <= late <= LAST and late not in DIRECT:
            arrived(twos[late])
            crossing += rest_across(late)
        if k - 1 in SPLIT:
            crossing += places_across(k - 1, pl.ds(0, 2), 3)
        step = k - A_LAG
        if step == 0:
            arrived(a_small)
            z_moves[2, 0, 1] = z_forward(2, 0, 0)
            z_moves[2, 1, 1] = z_forward(2, 0, 1)
        z_step(2, 0, step)
        z_step(2, 1, step)
        if 0 <= step <= LAST:
            crossing += a_across(step)
        if k == 1:
            s_arrived(s_moves)
            s_moves = [s_shift(2, 1, 0, 1), s_shift(2, -1, 0, 1)]
        if k == 3:
            s_arrived(s_moves)
            s_moves = [s_shift(3, 3, -1, 3), s_shift(3, -3, -1, 3)]
        if k == 5:
            s_arrived(s_moves)
            s_moves = [s_shift(4, 4, 1, 3), s_shift(4, -4, -4, 4)]
        if k == 7:
            s_arrived(s_moves)
            got_s = load(9, S, S_sm)
        if k == 8:
            got_s.wait()

    arrived(crossing)

    flat = G.reshape(512, BLK, BLK)

    def chunk_dot(s, count):
        left = jnp.concatenate([vals[s + i] for i in range(count)], axis=1)
        right = jnp.concatenate([flat[index[s + i]] for i in range(count)], axis=0)
        return jnp.dot(left, right, preferred_element_type=jnp.float32)

    total = chunk_dot(0, CHUNK)
    hidden = total.astype(jnp.bfloat16)
    got_grad.wait()
    grad = lax.dot_general(hidden, grad_out[...], (((0,), (0,)), ((), ())), preferred_element_type=jnp.float32)
    for i in range(16):
        W[i] = grad[8 * i : 8 * i + 8]

    me = x * 4 + y
    owner = c == 1
    plane = sorted(
        ((dx, dy) for dx in range(4) for dy in range(4)),
        key=lambda d: -min(d[0], 4 - d[0]) - min(d[1], 4 - d[1]),
    )

    def at_strip(i):
        return wgrad_hbm.at[pl.ds(pl.multiple_of(8 * i, 8), 8)]

    def strip_send(src, dst, sem, peer):
        pltpu.make_async_remote_copy(
            src_ref=src, dst_ref=dst, send_sem=sent_sem.at[2], recv_sem=sem,
            device_id=peer, device_id_type=MESH,
        ).start()

    def wait_strips(sem, count):
        wait_rows(sem, 32 * count)

    for j, (dx, dy) in enumerate(plane):
        px, py = (x + dx) % 4, (y + dy) % 4

        def scatter(px=px, py=py, j=j):
            strip_send(W.at[px * 4 + py], R1.at[2 * j + c], r_recv.at[0], device(z, px, 1, py))

        if dx or dy:
            scatter()
        else:
            pl.when(c == 0)(scatter)

    @pl.when(owner)
    def _():
        R1[31] = W[me]
        wait_strips(r_recv.at[0], 31)
        R2[0] = jnp.sum(R1[...], axis=0)
        for j in (8, 7, 9, 6, 10, 5, 11, 4, 12, 3, 13, 2, 14, 1, 15):
            strip_send(R2.at[0], R2.at[j], r_recv.at[1], device(z + j, x, c, y))

    got_weight.wait()
    layer[...] = jnp.dot(hidden, weight[...], preferred_element_type=jnp.float32).astype(jnp.bfloat16)
    put_layer = load(0, layer, layer_hbm)
    s_wait(s_sent.at[0], sum(s_rows))
    wait_rows(sent_sem.at[0], sum(sent_rows))
    wait_rows(sent_sem.at[1], sum(rows for _, rows in crossing))
    put_layer.wait()

    @pl.when(owner)
    def _():
        wait_strips(r_recv.at[1], 15)
        total_strip[...] = jnp.sum(R2[...], axis=0)
        for dx, dy in plane:
            px, py = (x + dx) % 4, (y + dy) % 4
            strip_send(total_strip, at_strip(me), r_recv.at[2], device(z, px, 0, py))
            if dx or dy:
                strip_send(total_strip, at_strip(me), r_recv.at[2], device(z, px, 1, py))
        put_strip = load(1, total_strip, at_strip(me))
        put_strip.wait()
        wait_strips(r_recv.at[2], 15)
        wait_strips(sent_sem.at[2], 15 + 15 + 31)

    @pl.when(c == 0)
    def _():
        wait_strips(r_recv.at[2], 16)
        wait_strips(sent_sem.at[2], 16)


def hand_over(layer_from, wgrad_from, layer_to, wgrad_to, layer, wgrad, sem):
    fetch = [
        pltpu.make_async_copy(layer_from, layer, sem.at[0]),
        pltpu.make_async_copy(wgrad_from, wgrad, sem.at[1]),
    ]
    store = [
        pltpu.make_async_copy(layer, layer_to, sem.at[2]),
        pltpu.make_async_copy(wgrad, wgrad_to, sem.at[3]),
    ]
    for copy in fetch:
        copy.start()
    for copy, then in zip(fetch, store):
        copy.wait()
        then.start()
    for copy in store:
        copy.wait()


def per_device(features, block_vals, block_cols, block_counts, hub_parts, send_blocks, weight, grad_out):
    dma = pltpu.SemaphoreType.DMA
    anywhere = pl.BlockSpec(memory_space=pl.ANY)
    outs = (
        jax.ShapeDtypeStruct((BLK, HID), jnp.bfloat16),
        jax.ShapeDtypeStruct((BLK, HID), jnp.float32),
    )
    results = pl.pallas_call(
        kernel,
        out_shape=outs,
        in_specs=[anywhere] * 8,
        out_specs=(anywhere,) * 2,
        scratch_shapes=[
            pltpu.VMEM((2, 8, 2, 4, 4, BLK, BLK), jnp.bfloat16),
            pltpu.VMEM((16, 2, 4, 1, BLK), jnp.int32),
            pltpu.SMEM((16, 2, 4, 1, BLK), jnp.int32),
            pltpu.VMEM((K, BLK, BLK), jnp.bfloat16),
            pltpu.SMEM((1, K), jnp.int32),
            pltpu.VMEM((1, K), jnp.int32),
            pltpu.SMEM((2,), jnp.int32),
            pltpu.VMEM((BLK, HID), jnp.bfloat16),
            pltpu.VMEM((BLK, HID), jnp.bfloat16),
            pltpu.VMEM((1, K), jnp.float32),
            pltpu.SMEM((1, K), jnp.float32),
            pltpu.SMEM((K,), jnp.int32),
            pltpu.SMEM((K,), jnp.int32),
            pltpu.SMEM((K,), jnp.int32),
            pltpu.VMEM((BLK, HID), jnp.bfloat16),
            pltpu.VMEM((16, 8, HID), jnp.float32),
            pltpu.VMEM((32, 8, HID), jnp.float32),
            pltpu.VMEM((16, 8, HID), jnp.float32),
            pltpu.VMEM((8, HID), jnp.float32),
            dma((10,)), dma((3,)), dma((5,)), dma((3, 2, LAST)), dma((2, 2, LAST + 1)), dma((LAST,)),
            dma((1,)), dma((1,)), dma((5,)), dma((3,)),
        ],
        compiler_params=pltpu.CompilerParams(
            collective_id=0, has_side_effects=True, vmem_limit_bytes=VMEM_BYTES
        ),
    )(features, block_vals, block_cols, block_counts, hub_parts, send_blocks, weight, grad_out)
    return pl.pallas_call(
        hand_over,
        out_shape=outs,
        in_specs=[anywhere] * 2,
        out_specs=(anywhere,) * 2,
        scratch_shapes=[pltpu.VMEM((BLK, HID), jnp.bfloat16), pltpu.VMEM((BLK, HID), jnp.float32), dma((4,))],
        compiler_params=pltpu.CompilerParams(vmem_limit_bytes=VMEM_BYTES),
    )(*results)


def solution(mesh):
    placed = (
        P(("nodes", "feat"), None),
        P(("nodes", "feat"), None, None, None),
        P(("nodes", "feat"), None),
        P(("nodes", "feat"), None),
        P(),
        P(("nodes", "feat"), None),
        P(),
        P(("nodes", "feat"), None),
    )
    return jax.shard_map(
        per_device,
        mesh=mesh,
        in_specs=placed,
        out_specs=(P(("nodes", "feat"), None), P()),
        check_vma=False,
    )
```
